256 devices in a mesh: src: 32 (over z, y_lo, core), slab: 8 (over x, y_hi).
Axes of the slice: x: 4, y: 4 (y_hi: 2, y_lo: 2; y = y_hi * 2 + y_lo), z: 8, core: 2. Of those that a mesh axis runs over, the one named last changes fastest.
Arguments:
- forward_field: float32 [32, 32, 384, 384], P('src', 'slab'), may hold values from -6 to 6
- misfit: float32 [32, 9216], P('src', 'slab'), may hold values from -6 to 6
- receivers: int32 [32, 9216, 2], P('src', 'slab'), may hold values from 0 to 147455, as said below
- classes: int32 [32, 384, 384], P('slab'), may hold values from 0 to 15
- table: float32 [16], replicated, may hold values from 0.3 to 3
Outputs:
- adjoint_field: float32 [32, 32, 384, 384], P('src', 'slab')
- gradient: float32 [32, 384, 384], P('slab', 'src')
The draws below stay inside these ranges and needn't reach their ends.
Inputs may be any that keep to these rules, and one draw needn't show every extreme that they name: `receivers`: entries of block k of 1152 entries along the second dimension have a first coordinate z with k * 4 <= z < (k + 1) * 4, and an index within the layer from 0 to 147455; the same cell may appear several times.
All inputs are finite; a program needn't handle non-finite values.
Results may differ from the reference program's by a relative error of at most 0.0003.
Values sent between devices are 32-bit elements; how exact they have to be, the bound alone decides.
No kernel may reach another device: no remote copies, remote signals or barrier semaphores. Data moves between devices by JAX's collectives and lax.ppermute only.
A program may use at most 128 MiB of HBM per device.

```python
import math
import jax
import jax.numpy as jnp
from jax import lax

CZ = 4
NY = 384
NX = 384
NCLASS = 16
ITERS = 3
SOURCES = 32
NZ = 32
RECV_DEV = 1152
RECV = 9216


def draw_receivers(key, part):
    key = jax.random.fold_in(key, 7)
    slabs = NZ // CZ
    layer_key, plane_key = jax.random.split(key)
    layers = jax.random.randint(layer_key, (SOURCES, slabs, RECV_DEV), 0, CZ, dtype=jnp.int32)
    layers = layers + (jnp.arange(slabs, dtype=jnp.int32) * CZ)[None, :, None]
    planes = jax.random.randint(plane_key, (SOURCES, slabs, RECV_DEV), 0, NY * NX, dtype=jnp.int32)
    layers = layers.at[0, 0, 0].set(0)
    planes = planes.at[0, 0, 0].set(0)
    layers = layers.at[SOURCES - 1, slabs - 1, RECV_DEV - 1].set(NZ - 1)
    planes = planes.at[SOURCES - 1, slabs - 1, RECV_DEV - 1].set(NY * NX - 1)
    entries = jnp.stack([layers, planes], axis=-1)
    return entries.reshape(SOURCES, slabs * RECV_DEV, 2)


def place_ends(values, rng, low, top_value):
    place = [jax.random.randint(jax.random.fold_in(rng, axis), (), 0, length) for axis, length in enumerate(values.shape)]
    main_axis = values.shape.index(max(values.shape))
    neighbour = place[:main_axis] + [(place[main_axis] + 1) % values.shape[main_axis]] + place[main_axis + 1:]
    return values.at[tuple(place)].set(low).at[tuple(neighbour)].set(top_value)


def spiked(values, key, source, target, blocks, factor):
    def block_of(axis_at):
        return (jnp.arange(values.shape[axis_at]) // (values.shape[axis_at] // blocks)).reshape((-1,) + (1,) * (values.ndim - 1 - axis_at))

    first = jax.random.permutation(key, blocks)[block_of(target)]
    second = (block_of(target) + blocks // 2) % blocks
    return jnp.where((block_of(source) == first) | (block_of(source) == second), factor * values, values)


def block_scale(key, shape, cuts, low, high):
    gain, own = 1.0, jax.random.fold_in(key, 6)
    for position, blocks in cuts:
        draws = jnp.exp(jax.random.uniform(jax.random.fold_in(own, position), (blocks,), jnp.float32, low / len(cuts), high / len(cuts)))
        gain = gain * jnp.repeat(draws, shape[position] // blocks).reshape([-1 if axis == position else 1 for axis in range(len(shape))])
    return gain


def normal_values(rng, extent, spread, limit, cuts=(), held_as=jnp.bfloat16):
    factor_of = block_scale(rng, extent, cuts, -0.22, 0.18) if cuts else 1.0
    array = jax.random.normal(rng, extent, jnp.float32) * spread * factor_of
    return jnp.minimum(jnp.maximum(array, -limit), limit).astype(held_as)


def gaussian_with(rng, dims, scale, bound, cuts, heavy, held_as=jnp.bfloat16):
    values = scale * jax.random.normal(rng, dims, jnp.float32)
    if cuts:
        values = values * block_scale(rng, dims, cuts, -0.22, 0.18)
    return jnp.clip(spiked(values, jax.random.fold_in(rng, 3), *heavy), -bound, bound).astype(held_as)


def setup_inputs(seed: int = 0) -> dict:
    key_list = jax.random.split(jax.random.key(seed), 6)
    forward_field = gaussian_with(key_list[0], (SOURCES, NZ, NY, NX), 1.0, 6.0, ((0, 32), (1, 8)), (0, 2, 32, 2.75), jnp.float32)
    misfit = normal_values(key_list[1], (SOURCES, RECV), 1.0, 6.0, ((0, 32), (1, 8)), jnp.float32)
    receivers = draw_receivers(jax.random.fold_in(key_list[5], 71), 0)
    classes = place_ends(jax.random.randint(key_list[3], (NZ, NY, NX), 0, NCLASS), jax.random.fold_in(key_list[3], 1), 0, NCLASS - 1).astype(jnp.int32)
    table = jnp.clip(jnp.exp(jax.random.uniform(key_list[4], (NCLASS,), jnp.float32, math.log(0.3), math.log(3.0))), 0.3, 3.0)
    return dict(forward_field=forward_field, misfit=misfit, receivers=receivers, classes=classes, table=table)


def neighbours(field):
    padded = jnp.pad(field, 1)
    return [padded[2:, 1:-1, 1:-1], padded[:-2, 1:-1, 1:-1],
            padded[1:-1, 2:, 1:-1], padded[1:-1, :-2, 1:-1],
            padded[1:-1, 1:-1, 2:], padded[1:-1, 1:-1, :-2]]


def reference(forward_field, misfit, receivers, classes, table):
    conduct = table[classes]
    couplings = [0.5 * (conduct + beside) for beside in neighbours(conduct)]
    diagonal = couplings[0]
    for coupling in couplings[1:]:
        diagonal = diagonal + coupling

    def operate(field):
        result = diagonal * field
        for coupling, beside in zip(couplings, neighbours(field)):
            result = result - coupling * beside
        return result

    def one_source(total, inputs):
        forward, values, pairs = inputs
        cells = (pairs[:, 0] * (NY * NX) + pairs[:, 1]).astype(jnp.int32)
        right_side = jnp.zeros((NZ * NY * NX,), jnp.float32).at[cells].add(values).reshape(NZ, NY, NX)
        adjoint = jnp.zeros_like(right_side)
        residual = right_side
        precond = residual / diagonal
        direction = precond
        inner_rz = jnp.sum(residual * precond)
        for number in range(ITERS):
            image = operate(direction)
            step_size = inner_rz / jnp.sum(direction * image)
            adjoint = adjoint + step_size * direction
            residual = residual - step_size * image
            precond = residual / diagonal
            inner_new = jnp.sum(residual * precond)
            direction = precond + (inner_new / inner_rz) * direction
            inner_rz = inner_new
        term = jnp.zeros_like(right_side)
        for forward_near, adjoint_near in zip(neighbours(forward), neighbours(adjoint)):
            term = term + (forward - forward_near) * (adjoint - adjoint_near)
        return total + term, adjoint

    start = jnp.zeros((NZ, NY, NX), jnp.float32)
    total, adjoint_field = lax.scan(one_source, start, (forward_field, misfit, receivers))
    return adjoint_field, -0.5 * total
```

```python
import jax
import jax.numpy as jnp
from jax import lax
from jax.sharding import PartitionSpec as P

CORES = 2
Y_LO = 2


def lookup(classes, table):
    result = jnp.zeros(classes.shape, jnp.float32)
    for label in range(table.shape[0]):
        result = jnp.where(classes == label, table[label], result)
    return result


def slab_shift(value, step):
    count = lax.axis_size("slab")
    pairs = [(i, i + step) for i in range(count) if 0 <= i + step < count]
    return lax.ppermute(value, "slab", pairs)


def shifted(field, dim, step):
    spread = [(0, 0)] * field.ndim
    size = field.shape[dim]
    if step > 0:
        spread[dim] = (0, 1)
        return lax.slice_in_dim(jnp.pad(field, spread), 1, size + 1, axis=dim)
    spread[dim] = (1, 0)
    return lax.slice_in_dim(jnp.pad(field, spread), 0, size, axis=dim)


def near(field):
    inner = field[1:-1]
    return [
        field[2:],
        field[:-2],
        shifted(inner, 1, 1),
        shifted(inner, 1, -1),
        shifted(inner, 2, 1),
        shifted(inner, 2, -1),
    ]


def spread_sum(field, conduct):
    centre = conduct[1:-1]
    total = 0.0
    for value, beside in zip(near(field), near(conduct)):
        total = total + 0.5 * (centre + beside) * value
    return total


def weights(moments):
    m = [moments[i] / moments[0] for i in range(6)]
    g = [m[i] - m[i + 1] for i in range(5)]
    l10 = g[1] / g[0]
    l20 = g[2] / g[0]
    d1 = g[2] - l10 * g[1]
    e = g[3] - l20 * g[1]
    l21 = e / d1
    d2 = g[4] - l20 * g[2] - l21 * e
    y0 = m[0]
    y1 = m[1] - l10 * y0
    y2 = m[2] - l20 * y0 - l21 * y1
    c2 = y2 / d2
    c1 = y1 / d1 - l21 * c2
    c0 = y0 / g[0] - l10 * c1 - l20 * c2
    return c0, c1, c2


def body(forward_field, misfit, receivers, classes, table):
    layers, rows, columns = classes.shape
    sources = lax.axis_size("src")
    per_z = CORES * Y_LO
    depth = sources // per_z
    place = lax.axis_index("src")
    core = place % CORES
    slab = lax.axis_index("slab")
    blocks = depth * CORES
    strip = rows // blocks
    forward = forward_field[0]

    mine = (place // per_z) * CORES + core
    part = lookup(lax.dynamic_slice_in_dim(classes, mine * strip, strip, axis=1), table)
    below = slab_shift(part, 1)
    above = slab_shift(part, -1)
    groups = [
        [z * per_z + y * CORES + c for z in range(depth) for c in range(CORES)] for y in range(Y_LO)
    ]
    halo = lax.all_gather(jnp.stack([below, above]), "src", axis_index_groups=groups)
    halo = jnp.moveaxis(halo, 0, 2).reshape(2, layers, rows, columns)
    conduct = jnp.concatenate([halo[0], lookup(classes, table), halo[1]], axis=0)

    forward_pad = jnp.concatenate(
        [slab_shift(forward[-1:], 1), forward, slab_shift(forward[:1], -1)], axis=0
    )

    pairs = receivers[0].T.astype(jnp.float32)
    entries = jnp.concatenate([pairs, misfit], axis=0)
    entries = jnp.concatenate([slab_shift(entries, 1), entries, slab_shift(entries, -1)], axis=1)
    first = entries[0].astype(jnp.int32) - slab * layers + 3
    inside = (first >= 0) & (first < layers + 6)
    cells = first * (rows * columns) + entries[1].astype(jnp.int32)
    size = (layers + 6) * rows * columns
    right_side = (
        jnp.zeros((size,), jnp.float32)
        .at[jnp.where(inside, cells, size)]
        .add(entries[2], mode="drop")
        .reshape(layers + 6, rows, columns)
    )

    centre = conduct[1:-1]
    diagonal = 0.0
    for beside in near(conduct):
        diagonal = diagonal + 0.5 * (centre + beside)
    layer = jnp.arange(-3, layers + 3) + slab * layers
    real = ((layer >= 0) & (layer < layers * lax.axis_size("slab")))[:, None, None]
    inverse = jnp.where(real, 1.0 / jnp.where(real, diagonal, 1.0), 0.0)
    first_field = right_side * inverse
    spread0 = spread_sum(first_field, conduct[1:-1])
    second_field = spread0 * inverse[1:-1]
    spread1 = spread_sum(second_field, conduct[2:-2])
    third_field = spread1 * inverse[2:-2]
    spread2 = spread_sum(third_field, conduct[3:-3])
    own0, own1, own2 = first_field[3:-3], second_field[2:-2], third_field[1:-1]
    sums = jnp.stack(
        [
            jnp.sum(own0 * right_side[3:-3]),
            jnp.sum(own0 * spread0[2:-2]),
            jnp.sum(own1 * spread0[2:-2]),
            jnp.sum(own1 * spread1[1:-1]),
            jnp.sum(own2 * spread1[1:-1]),
            jnp.sum(own2 * spread2),
        ]
    )
    count = lax.axis_size("slab")
    sums = lax.all_to_all(jnp.broadcast_to(sums, (count, 6)), "slab", 0, 0)
    c0, c1, c2 = weights(jnp.sum(sums, axis=0))
    adjoint = c0 * first_field[2:-2] + c1 * second_field[1:-1] + c2 * third_field
    forward_near = near(forward_pad)
    adjoint_near = near(adjoint)
    adjoint = adjoint[1:-1]
    term = 0.0
    for forward_side, adjoint_side in zip(forward_near, adjoint_near):
        term = term + (forward - forward_side) * (adjoint - adjoint_side)
    term = -0.5 * term

    own = rows // sources
    term = term.reshape(layers, depth * Y_LO, CORES, own, columns)
    term = jnp.transpose(term, (2, 1, 0, 3, 4)).reshape(CORES, depth * Y_LO, layers * own, columns)
    keep = lax.dynamic_index_in_dim(term, core, 0, keepdims=False)
    give = lax.dynamic_index_in_dim(term, 1 - core, 0, keepdims=False)
    got = lax.ppermute(give, "src", [(i, i ^ 1) for i in range(sources)])
    half = keep + got
    groups = [
        [z * per_z + y * CORES + c for z in range(depth) for y in range(Y_LO)] for c in range(CORES)
    ]
    shares = lax.all_to_all(half, "src", 0, 0, axis_index_groups=groups)
    gradient = jnp.sum(shares, axis=0).reshape(layers, own, columns)
    return (adjoint[None], gradient)


def solution(mesh):
    placed = (
        P("src", "slab", None, None),
        P("src", "slab"),
        P("src", "slab", None),
        P("slab", None, None),
        P(),
    )
    return jax.shard_map(
        body,
        mesh=mesh,
        in_specs=placed,
        out_specs=(P("src", "slab", None, None), P("slab", "src", None)),
        check_vma=False,
    )
```

```python
import jax
import jax.numpy as jnp
from jax import lax
from jax.experimental import pallas as pl
from jax.experimental.pallas import tpu as pltpu
from jax.sharding import PartitionSpec as P

CORES = 2
Y_LO = 2
REACH = 3
PAD = 8
ROWS = 96
GROUP = 4
VMEM = 56 * 1024 * 1024


def lookup(classes, table):
    labels = jnp.arange(table.shape[0], dtype=jnp.int32)[:, None, None, None]
    return jnp.sum(jnp.where(classes[None] == labels, table[:, None, None, None], 0.0), axis=0)


def slab_shift(value, step):
    count = lax.axis_size("slab")
    pairs = [(i, i + step) for i in range(count) if 0 <= i + step < count]
    return lax.ppermute(value, "slab", pairs)


def scatter_kernel(below, own, above, classes, table, side, conduct):
    layers, rows, columns = classes.shape
    slab = lax.axis_index("slab")
    count = own.shape[1]
    across = lax.broadcasted_iota(jnp.int32, (columns, count), 0)
    down = lax.broadcasted_iota(jnp.int32, (rows, count), 0)
    sources = (
        (below, range(layers - REACH, layers), 0),
        (own, range(layers), REACH),
        (above, range(REACH), REACH + layers),
    )
    for number, (entries, planes, start) in enumerate(sources):
        first = entries[0:1, :] - ((slab + number - 1) * layers).astype(jnp.float32)
        index = entries[1:2, :]
        value = entries[2:3, :]
        line = jnp.floor((index + 0.5) * (1.0 / columns))
        column = (index - line * columns).astype(jnp.int32)
        place = (first * rows + line).astype(jnp.int32)
        hit = across == column
        parts = []
        rest = value
        for _ in range(3):
            piece = rest.astype(jnp.bfloat16)
            rest = rest - piece.astype(jnp.float32)
            parts.append(jnp.where(hit, piece.astype(jnp.float32), 0.0).astype(jnp.bfloat16))
        for step, plane in enumerate(planes):
            chosen = jnp.where(down + plane * rows == place, 1.0, 0.0).astype(jnp.bfloat16)
            total = 0.0
            for part in parts:
                total = total + lax.dot_general(
                    chosen, part, (((1,), (1,)), ((), ())), preferred_element_type=jnp.float32
                )
            side[start + step] = total

    values = [table[label] for label in range(table.shape[0])]

    def strip(at, carry):
        at = pl.multiple_of(at * ROWS, ROWS)
        for layer in range(layers):
            conduct[layer, pl.ds(at, ROWS), :] = choose(classes[layer, pl.ds(at, ROWS), :], values)
        return carry

    lax.fori_loop(0, rows // ROWS, strip, 0)


def choose(labels, values):
    bit = 1
    while len(values) > 1:
        high = (labels & bit) != 0
        values = [jnp.where(high, values[i + 1], values[i]) for i in range(0, len(values), 2)]
        bit *= 2
    return values[0]


def vectors_kernel(own, halo, side, out0, out1, out2, sums, cond, near_x, near_y, near_z, inverse, f0, f1, f2, marks):
    layers, rows, columns = own.shape
    blocks, _, _, strip, _ = halo.shape
    filled = pl.ds(PAD, rows)
    copies = [
        pltpu.make_async_copy(own, cond.at[pl.ds(layers, layers), filled], marks.at[0])
    ]
    for block in range(blocks):
        for step in range(2):
            target = cond.at[pl.ds(2 * step * layers, layers), pl.ds(PAD + block * strip, strip)]
            copies.append(
                pltpu.make_async_copy(halo.at[block, step], target, marks.at[len(copies)])
            )
    for copy in copies:
        copy.start()
    slab = lax.axis_index("slab")
    slabs = lax.axis_size("slab")
    deep = layers + 2 * REACH
    lane = lax.broadcasted_iota(jnp.int32, (ROWS, columns), 1)
    blank = jnp.zeros((PAD, columns), jnp.float32)
    for ref in (cond, near_y, f0, f1, f2):
        for plane in range(ref.shape[0]):
            ref[plane, 0:PAD, :] = blank
            ref[plane, PAD + rows : 2 * PAD + rows, :] = blank
    for copy in copies:
        copy.wait()

    def here(at):
        return pl.ds(pl.multiple_of(at * ROWS + PAD, PAD), ROWS)

    def before(at):
        return pl.ds(pl.multiple_of(at * ROWS, PAD), ROWS + PAD)

    def after(at):
        return pl.ds(pl.multiple_of(at * ROWS + PAD, PAD), ROWS + PAD)

    def plain(at):
        return pl.ds(pl.multiple_of(at * ROWS, ROWS), ROWS)

    strips = rows // ROWS

    def setup(plane, carry):
        layer = slab * layers + plane - REACH
        real = jnp.logical_and(layer >= 0, layer < slabs * layers)
        scale = jnp.where(real, 1.0, 0.0)

        def step(at, inner):
            centre = cond[plane + 1, here(at), :]
            lower = cond[plane, here(at), :]
            upper = cond[plane + 2, here(at), :]
            ahead = cond[plane + 1, after(at), :][1 : ROWS + 1]
            behind = cond[plane + 1, before(at), :][PAD - 1 : PAD - 1 + ROWS]
            right = jnp.where(lane == columns - 1, 0.0, pltpu.roll(centre, columns - 1, 1))
            left = jnp.where(lane == 0, 0.0, pltpu.roll(centre, 1, 1))
            total = 6.0 * centre + ((lower + upper) + (ahead + behind) + (left + right))
            turned = (2.0 * scale) / (total + (1.0 - scale))
            inverse[plane, plain(at), :] = turned
            near_x[plane, plain(at), :] = jnp.where(lane == columns - 1, 0.0, 0.5 * (centre + right))
            near_y[plane, here(at), :] = 0.5 * (centre + ahead)
            near_z[plane, plain(at), :] = 0.5 * (centre + upper)
            f0[plane, here(at), :] = side[plane, plain(at), :] * turned
            return inner

        return lax.fori_loop(0, strips, step, carry)

    lax.fori_loop(0, deep, setup, 0)
    thick = layers + 2
    write0 = pltpu.make_async_copy(f0.at[pl.ds(2, thick), filled], out0, marks.at[0])
    write0.start()

    def spread(field, offset, plane, at):
        centre = field[plane, here(at), :]
        across = near_x[plane + offset, plain(at), :]
        total = across * pltpu.roll(centre, columns - 1, 1) + pltpu.roll(across * centre, 1, 1)
        ahead = field[plane, after(at), :][1 : ROWS + 1]
        total = total + near_y[plane + offset, here(at), :] * ahead
        behind = near_y[plane + offset, before(at), :] * field[plane, before(at), :]
        total = total + behind[PAD - 1 : PAD - 1 + ROWS]
        total = total + near_z[plane + offset, plain(at), :] * field[plane + 1, here(at), :]
        total = total + near_z[plane + offset - 1, plain(at), :] * field[plane - 1, here(at), :]
        return centre, total

    def fold(value):
        total = value[0:8]
        for start in range(8, ROWS, 8):
            total = total + value[start : start + 8]
        return total

    def outer(field, offset, target, planes):
        for plane in planes:

            def step(at, inner, plane=plane):
                _, total = spread(field, offset, plane, at)
                target[plane - 1, here(at), :] = total * inverse[plane + offset, plain(at), :]
                return inner

            lax.fori_loop(0, strips, step, 0)

    zero = jnp.zeros((8, columns), jnp.float32)

    def inside0(plane, carry):
        def step(at, inner):
            s0, s1, s2 = inner
            centre, total = spread(f0, 0, plane, at)
            value = total * inverse[plane, plain(at), :]
            f1[plane - 1, here(at), :] = value
            return (
                s0 + fold(centre * side[plane, plain(at), :]),
                s1 + fold(centre * total),
                s2 + fold(value * total),
            )

        return lax.fori_loop(0, strips, step, carry)

    def inside1(plane, carry):
        def step(at, inner):
            s3, s4 = inner
            centre, total = spread(f1, 1, plane, at)
            value = total * inverse[plane + 1, plain(at), :]
            f2[plane - 1, here(at), :] = value
            return s3 + fold(centre * total), s4 + fold(value * total)

        return lax.fori_loop(0, strips, step, carry)

    def inside2(plane, carry):
        def step(at, inner):
            centre, total = spread(f2, 2, plane, at)
            return inner + fold(centre * total)

        return lax.fori_loop(0, strips, step, carry)

    outer(f0, 0, f1, (1, 2, deep - 3, deep - 2))
    s0, s1, s2 = lax.fori_loop(REACH, REACH + layers, inside0, (zero, zero, zero))
    write1 = pltpu.make_async_copy(f1.at[pl.ds(1, thick), filled], out1, marks.at[1])
    write1.start()
    outer(f1, 1, f2, (1, deep - 4))
    s3, s4 = lax.fori_loop(REACH - 1, REACH - 1 + layers, inside1, (zero, zero))
    write2 = pltpu.make_async_copy(f2.at[:, filled], out2, marks.at[2])
    write2.start()
    s5 = lax.fori_loop(REACH - 2, REACH - 2 + layers, inside2, zero)
    for row, total in enumerate((s0, s1, s2, s3, s4, s5)):
        single = jnp.sum(jnp.sum(total, axis=0, keepdims=True), axis=1, keepdims=True)
        sums[row : row + 1, :] = jnp.broadcast_to(single, (1, sums.shape[1]))
    sums[6:8, :] = jnp.zeros((2, sums.shape[1]), jnp.float32)
    for copy in (write0, write1, write2):
        copy.wait()


def weights(moments):
    m = [moments[i] / moments[0] for i in range(6)]
    g = [m[i] - m[i + 1] for i in range(5)]
    l10 = g[1] / g[0]
    l20 = g[2] / g[0]
    d1 = g[2] - l10 * g[1]
    e = g[3] - l20 * g[1]
    l21 = e / d1
    d2 = g[4] - l20 * g[2] - l21 * e
    y0 = m[0]
    y1 = m[1] - l10 * y0
    y2 = m[2] - l20 * y0 - l21 * y1
    c2 = y2 / d2
    c1 = y1 / d1 - l21 * c2
    c0 = y0 / g[0] - l10 * c1 - l20 * c2
    return c0, c1, c2


def terms_kernel(sums, w0, w1, w2, forward, lower, upper, adjoint, keep, give, adj, fwd):
    layers, rows, columns = forward.shape
    pairs, _, _ = keep.shape
    strip = rows // pairs
    half = strip // 2
    first = lax.axis_index("src") % CORES == 0
    blank = jnp.zeros((PAD, columns), jnp.float32)
    for ref in (adj, fwd):
        for plane in range(layers + 2):
            ref[plane, 0:PAD, :] = blank
            ref[plane, PAD + rows : 2 * PAD + rows, :] = blank
    fwd[0, PAD : PAD + rows, :] = lower[0]
    fwd[layers + 1, PAD : PAD + rows, :] = upper[0]
    total = sums[0]
    for other in range(1, sums.shape[0]):
        total = total + sums[other]
    c0, c1, c2 = weights([total[i : i + 1, 0:1] for i in range(6)])
    c0, c1, c2 = [jnp.broadcast_to(c, (ROWS, columns)) for c in (c0, c1, c2)]

    for plane in range(layers + 2):

        def mix(at, carry, plane=plane):
            span = pl.ds(pl.multiple_of(at * ROWS, ROWS), ROWS)
            wide = pl.ds(pl.multiple_of(at * ROWS + PAD, PAD), ROWS)
            value = c0 * w0[plane, span, :] + c1 * w1[plane, span, :] + c2 * w2[plane, span, :]
            adj[plane, wide, :] = value
            if 0 < plane <= layers:
                adjoint[plane - 1, span, :] = value
                fwd[plane, wide, :] = forward[plane - 1, span, :]
            return carry

        lax.fori_loop(0, rows // ROWS, mix, 0)

    tall = strip * GROUP
    lane = lax.broadcasted_iota(jnp.int32, (tall, columns), 1)
    last = lane == columns - 1
    start = lane == 0

    def ahead(value):
        return jnp.where(last, 0.0, pltpu.roll(value, columns - 1, 1))

    for layer in range(layers):

        def step(at, carry, layer=layer):
            wide = pl.ds(pl.multiple_of(at * tall + PAD, PAD), tall)
            more = pl.ds(pl.multiple_of(at * tall, PAD), tall + 2 * PAD)
            f_all = fwd[layer + 1, more, :]
            a_all = adj[layer + 1, more, :]
            f = f_all[PAD : PAD + tall]
            a = a_all[PAD : PAD + tall]
            edge = (f - ahead(f)) * (a - ahead(a))
            value = edge + jnp.where(start, f * a, pltpu.roll(edge, 1, 1))
            for plane in (layer, layer + 2):
                value = value + (f - fwd[plane, wide, :]) * (a - adj[plane, wide, :])
            for shift in (PAD - 1, PAD + 1):
                span = slice(shift, shift + tall)
                value = value + (f - f_all[span]) * (a - a_all[span])
            value = -0.5 * value
            for number in range(GROUP):
                top = value[number * strip : number * strip + half]
                bottom = value[number * strip + half : (number + 1) * strip]
                block = at * GROUP + number
                keep[block, layer * half : (layer + 1) * half, :] = jnp.where(first, top, bottom)
                give[block, layer * half : (layer + 1) * half, :] = jnp.where(first, bottom, top)
            return carry

        lax.fori_loop(0, pairs // GROUP, step, 0)


def body(forward_field, misfit, receivers, classes, table):
    layers, rows, columns = classes.shape
    sources = lax.axis_size("src")
    count = lax.axis_size("slab")
    per_z = CORES * Y_LO
    depth = sources // per_z
    place = lax.axis_index("src")
    core = place % CORES
    blocks = depth * CORES
    strip = rows // blocks
    forward = forward_field[0]
    params = pltpu.CompilerParams(vmem_limit_bytes=VMEM)

    def struct(*shape):
        return jax.ShapeDtypeStruct(shape, jnp.float32)

    mine = (place // per_z) * CORES + core
    part = lookup(lax.dynamic_slice_in_dim(classes, mine * strip, strip, axis=1), table)
    from_below = slab_shift(part, 1)
    from_above = slab_shift(part, -1)
    groups = [
        [z * per_z + y * CORES + c for z in range(depth) for c in range(CORES)] for y in range(Y_LO)
    ]
    halo = lax.all_gather(jnp.stack([from_below, from_above]), "src", axis_index_groups=groups)

    entries = jnp.concatenate([receivers[0].T.astype(jnp.float32), misfit], axis=0)
    below = slab_shift(entries, 1)
    above = slab_shift(entries, -1)
    bottom, top, below, above = lax.optimization_barrier(
        (forward[:1], forward[-1:], below, above)
    )
    lower = slab_shift(top, 1)
    upper = slab_shift(bottom, -1)

    vmem = pl.BlockSpec(memory_space=pltpu.VMEM)
    anywhere = pl.BlockSpec(memory_space=pl.ANY)
    smem = pl.BlockSpec(memory_space=pltpu.SMEM)
    deep = layers + 2 * REACH
    side, own = pl.pallas_call(
        scatter_kernel,
        out_shape=(struct(deep, rows, columns), struct(layers, rows, columns)),
        in_specs=[vmem, vmem, vmem, vmem, smem],
        compiler_params=params,
        name="scatter",
    )(below, entries, above, classes, table)

    tall = rows + 2 * PAD
    thick = layers + 2
    w0, w1, w2, sums = pl.pallas_call(
        vectors_kernel,
        out_shape=(struct(thick, rows, columns),) * 3 + (struct(8, 128),),
        in_specs=[anywhere, anywhere, vmem],
        out_specs=(anywhere, anywhere, anywhere, vmem),
        scratch_shapes=[
            pltpu.VMEM((deep + 2, tall, columns), jnp.float32),
            pltpu.VMEM((deep, rows, columns), jnp.float32),
            pltpu.VMEM((deep, tall, columns), jnp.float32),
            pltpu.VMEM((deep, rows, columns), jnp.float32),
            pltpu.VMEM((deep, rows, columns), jnp.float32),
            pltpu.VMEM((deep, tall, columns), jnp.float32),
            pltpu.VMEM((deep - 2, tall, columns), jnp.float32),
            pltpu.VMEM((deep - 4, tall, columns), jnp.float32),
            pltpu.SemaphoreType.DMA((2 * blocks + 1,)),
        ],
        compiler_params=params,
        name="vectors",
    )(own, halo, side)

    sums = lax.all_to_all(jnp.broadcast_to(sums[None], (count, 8, 128)), "slab", 0, 0)
    half = rows // sources
    adjoint, keep, give = pl.pallas_call(
        terms_kernel,
        out_shape=(struct(layers, rows, columns),) + (struct(blocks, layers * half, columns),) * 2,
        scratch_shapes=[pltpu.VMEM((thick, tall, columns), jnp.float32)] * 2,
        compiler_params=params,
        name="terms",
    )(sums, w0, w1, w2, forward, lower, upper)

    got = lax.ppermute(give, "src", [(i, i ^ 1) for i in range(sources)])
    groups = [
        [z * per_z + y * CORES + c for z in range(depth) for y in range(Y_LO)] for c in range(CORES)
    ]
    shares = lax.all_to_all(keep + got, "src", 0, 0, axis_index_groups=groups)
    gradient = jnp.sum(shares, axis=0).reshape(layers, half, columns)
    return (adjoint[None], gradient)


def solution(mesh):
    placed = (
        P("src", "slab", None, None),
        P("src", "slab"),
        P("src", "slab", None),
        P("slab", None, None),
        P(),
    )
    return jax.shard_map(
        body,
        mesh=mesh,
        in_specs=placed,
        out_specs=(P("src", "slab", None, None), P("slab", "src", None)),
        check_vma=False,
    )
```

```python
import jax
import jax.numpy as jnp
from jax import lax
from jax.experimental import pallas as pl
from jax.experimental.pallas import tpu as pltpu
from jax.sharding import PartitionSpec as P

CORES = 2
Y_LO = 2
REACH = 3
PAD = 8
ROWS = 16
UNROLL = 24
GROUP = 2
PARTS = 8
PIECES = 3
MIB = 1024 * 1024


def lookup(classes, table):
    labels = jnp.arange(table.shape[0], dtype=jnp.int32)[:, None, None, None]
    return jnp.sum(jnp.where(classes[None] == labels, table[:, None, None, None], 0.0), axis=0)


def slab_ring(value, step):
    count = lax.axis_size("slab")
    return lax.ppermute(value, "slab", [(i, (i + step) % count) for i in range(count)])


def scatter_kernel(below, own, above, classes, table, side, conduct):
    layers, rows, columns = classes.shape
    slab = lax.axis_index("slab")
    count = own.shape[1] * PIECES
    across = lax.broadcasted_iota(jnp.int32, (count, columns), 1)
    down = lax.broadcasted_iota(jnp.int32, (rows, count), 0)
    sources = (
        (below, range(layers - REACH, layers), 0),
        (own, range(layers), REACH),
        (above, range(REACH), REACH + layers),
    )
    for number, (entries, planes, start) in enumerate(sources):
        top = entries.shape[0] - 3 * PIECES
        lines = [entries[row : row + 1, :] for row in range(top, entries.shape[0])]
        first, index, value = [
            jnp.concatenate(lines[at * PIECES : (at + 1) * PIECES], axis=1) for at in range(3)
        ]
        first = first - ((slab + number - 1) * layers).astype(jnp.float32)
        line = jnp.floor((index + 0.5) * (1.0 / columns))
        place = (first * rows + line).astype(jnp.int32)
        upright = jnp.transpose(
            jnp.concatenate([index - line * columns, value] + [value * 0.0] * 6, axis=0)
        )
        hit = across == upright[:, 0:1].astype(jnp.int32)
        parts = []
        rest = upright[:, 1:2]
        for _ in range(3):
            piece = rest.astype(jnp.bfloat16).astype(jnp.float32)
            rest = rest - piece
            parts.append(jnp.where(hit, piece, 0.0).astype(jnp.bfloat16))
        parts = jnp.concatenate(parts, axis=1)
        for step, plane in enumerate(planes):
            chosen = jnp.where(down + plane * rows == place, 1.0, 0.0).astype(jnp.bfloat16)
            total = jnp.dot(chosen, parts, preferred_element_type=jnp.float32)
            side[start + step] = (
                total[:, :columns] + total[:, columns : 2 * columns] + total[:, 2 * columns :]
            )

    values = [table[label] for label in range(table.shape[0])]

    def strip(at, carry):
        at = pl.multiple_of(at * ROWS, ROWS)
        for layer in range(layers):
            conduct[layer, pl.ds(at, ROWS), :] = choose(classes[layer, pl.ds(at, ROWS), :], values)
        return carry

    sweep(rows // ROWS, strip, 0)


def choose(labels, values):
    bit = 1
    while len(values) > 1:
        high = (labels & bit) != 0
        values = [jnp.where(high, values[i + 1], values[i]) for i in range(0, len(values), 2)]
        bit *= 2
    return values[0]


def sweep(count, step, carry, unroll=None):
    unroll = unroll or UNROLL

    def several(at, inner):
        for number in range(unroll):
            inner = step(at * unroll + number, inner)
        return inner

    return lax.fori_loop(0, count // unroll, several, carry)


def reciprocal(value):
    guess = pl.reciprocal(value, approx=True)
    for _ in range(2):
        guess = guess * (2.0 - value * guess)
    return guess


def vectors_kernel(
    own, halo, side, f0, f1, f2, sums, cond, near_x, near_y, near_z, inverse, marks
):
    layers, rows, columns = own.shape
    blocks, _, _, strip, _ = halo.shape
    filled = pl.ds(PAD, rows)
    first_copies, copies = [], []

    def fetch(source, target, group):
        mark = marks.at[len(first_copies) + len(copies)]
        copy = pltpu.make_async_copy(source, target, mark)
        copy.start()
        group.append(copy)

    fetch(own, cond.at[pl.ds(layers, layers), filled], first_copies)
    for block in range(blocks):
        for step in range(2):
            target = cond.at[pl.ds(2 * step * layers, layers), pl.ds(PAD + block * strip, strip)]
            fetch(halo.at[block, step], target, copies)
    slab = lax.axis_index("slab")
    slabs = lax.axis_size("slab")
    deep = layers + 2 * REACH
    lane = lax.broadcasted_iota(jnp.int32, (ROWS, columns), 1)
    blank = jnp.zeros((PAD, columns), jnp.float32)
    for ref in (cond, near_y, f0, f1, f2):
        for plane in range(ref.shape[0]):
            ref[plane, 0:PAD, :] = blank
            ref[plane, PAD + rows : 2 * PAD + rows, :] = blank

    def here(at):
        return pl.ds(pl.multiple_of(at * ROWS + PAD, PAD), ROWS)

    def before(at):
        return pl.ds(pl.multiple_of(at * ROWS, PAD), ROWS + PAD)

    def after(at):
        return pl.ds(pl.multiple_of(at * ROWS + PAD, PAD), ROWS + PAD)

    def plain(at):
        return pl.ds(pl.multiple_of(at * ROWS, ROWS), ROWS)

    strips = rows // ROWS

    def setup(plane, carry):
        layer = slab * layers + plane - REACH
        real = jnp.logical_and(layer >= 0, layer < slabs * layers)
        scale = jnp.where(real, 1.0, 0.0)

        def step(at, inner):
            centre = cond[plane + 1, here(at), :]
            lower = cond[plane, here(at), :]
            upper = cond[plane + 2, here(at), :]
            ahead = cond[plane + 1, after(at), :][1 : ROWS + 1]
            behind = cond[plane + 1, before(at), :][PAD - 1 : PAD - 1 + ROWS]
            right = jnp.where(lane == columns - 1, 0.0, pltpu.roll(centre, columns - 1, 1))
            left = jnp.where(lane == 0, 0.0, pltpu.roll(centre, 1, 1))
            total = 6.0 * centre + ((lower + upper) + (ahead + behind) + (left + right))
            turned = scale * reciprocal(total + (1.0 - scale))
            inverse[plane, plain(at), :] = turned
            near_x[plane, plain(at), :] = jnp.where(lane == columns - 1, 0.0, centre + right)
            near_y[plane, here(at), :] = centre + ahead
            near_z[plane, plain(at), :] = centre + upper
            f0[plane, here(at), :] = side[plane, plain(at), :] * (2.0 * turned)
            return inner

        return sweep(strips, step, carry)

    for copy in first_copies:
        copy.wait()
    lax.fori_loop(REACH + 1, REACH + layers - 1, setup, 0)
    for copy in copies:
        copy.wait()
    lax.fori_loop(0, REACH + 1, setup, 0)
    lax.fori_loop(REACH + layers - 1, deep, setup, 0)

    def spread(field, offset, plane, at):
        centre = field[plane, here(at), :]
        across = near_x[plane + offset, plain(at), :]
        total = across * pltpu.roll(centre, columns - 1, 1) + pltpu.roll(across * centre, 1, 1)
        ahead = field[plane, after(at), :][1 : ROWS + 1]
        total = total + near_y[plane + offset, here(at), :] * ahead
        behind = near_y[plane + offset, before(at), :] * field[plane, before(at), :]
        total = total + behind[PAD - 1 : PAD - 1 + ROWS]
        total = total + near_z[plane + offset, plain(at), :] * field[plane + 1, here(at), :]
        total = total + near_z[plane + offset - 1, plain(at), :] * field[plane - 1, here(at), :]
        return centre, total

    def fold(value):
        total = value[0:8]
        for start in range(8, ROWS, 8):
            total = total + value[start : start + 8]
        return total

    def outer(field, offset, target, planes):
        for plane in planes:

            def step(at, inner, plane=plane):
                _, total = spread(field, offset, plane, at)
                target[plane - 1, here(at), :] = total * inverse[plane + offset, plain(at), :]
                return inner

            sweep(strips, step, 0)

    zero = jnp.zeros((8, columns), jnp.float32)

    def inside0(plane, carry):
        def step(at, inner):
            s0, s1, s2 = inner
            centre, total = spread(f0, 0, plane, at)
            value = total * inverse[plane, plain(at), :]
            f1[plane - 1, here(at), :] = value
            return (
                s0 + fold(centre * side[plane, plain(at), :]),
                s1 + fold(centre * total),
                s2 + fold(value * total),
            )

        return sweep(strips, step, carry)

    def inside1(plane, carry):
        def step(at, inner):
            s3, s4 = inner
            centre, total = spread(f1, 1, plane, at)
            value = total * inverse[plane + 1, plain(at), :]
            f2[plane - 1, here(at), :] = value
            return s3 + fold(centre * total), s4 + fold(value * total)

        return sweep(strips, step, carry)

    def inside2(plane, carry):
        def step(at, inner):
            centre, total = spread(f2, 2, plane, at)
            return inner + fold(centre * total)

        return sweep(strips, step, carry)

    outer(f0, 0, f1, (1, 2, deep - 3, deep - 2))
    s0, s1, s2 = lax.fori_loop(REACH, REACH + layers, inside0, (zero, zero, zero))
    outer(f1, 1, f2, (1, deep - 4))
    s3, s4 = lax.fori_loop(REACH - 1, REACH - 1 + layers, inside1, (zero, zero))
    s5 = lax.fori_loop(REACH - 2, REACH - 2 + layers, inside2, zero)
    for row, total in enumerate((2.0 * s0, s1, s2, s3, s4, s5)):
        single = jnp.sum(jnp.sum(total, axis=0, keepdims=True), axis=1, keepdims=True)
        for target in range(sums.shape[0]):
            sums[target, row : row + 1, :] = jnp.broadcast_to(single, (1, sums.shape[2]))
    for target in range(sums.shape[0]):
        sums[target, 6:8, :] = jnp.zeros((2, sums.shape[2]), jnp.float32)


def weights(moments):
    m = [moments[i] / moments[0] for i in range(6)]
    g = [m[i] - m[i + 1] for i in range(5)]
    l10 = g[1] / g[0]
    l20 = g[2] / g[0]
    d1 = g[2] - l10 * g[1]
    e = g[3] - l20 * g[1]
    l21 = e / d1
    d2 = g[4] - l20 * g[2] - l21 * e
    y0 = m[0]
    y1 = m[1] - l10 * y0
    y2 = m[2] - l20 * y0 - l21 * y1
    c2 = y2 / d2
    c1 = y1 / d1 - l21 * c2
    c0 = y0 / g[0] - l10 * c1 - l20 * c2
    return c0, c1, c2


def terms_kernel(
    sums, w0, w1, w2, forward, lower, upper, adjoint, keep, give, adj, fwd, marks
):
    layers, rows, columns = forward.shape
    pairs, _, _ = keep.shape
    strip = rows // pairs
    half = strip // 2
    thick = layers + 2
    first = lax.axis_index("src") % CORES == 0
    slab = lax.axis_index("slab")
    filled = pl.ds(PAD, rows)
    fields = []
    for number, (source, start, count) in enumerate(
        ((lower, 0, 1), (forward, 1, layers), (upper, layers + 1, 1))
    ):
        target = fwd.at[pl.ds(start, count), filled]
        fields.append(pltpu.make_async_copy(source, target, marks.at[number]))
        fields[-1].start()
    blank = jnp.zeros((PAD, columns), jnp.float32)
    for ref in (adj, fwd):
        for plane in range(thick):
            ref[plane, 0:PAD, :] = blank
            ref[plane, PAD + rows : 2 * PAD + rows, :] = blank
    total = sums[0]
    for other in range(1, sums.shape[0]):
        total = total + sums[other]
    c0, c1, c2 = weights([total[i : i + 1, 0:1] for i in range(6)])
    c0, c1, c2 = [jnp.broadcast_to(c, (ROWS, columns)) for c in (c0, c1, c2)]

    written = []
    for plane in range(thick):
        def mix(at, carry, plane=plane):
            wide = pl.ds(pl.multiple_of(at * ROWS + PAD, PAD), ROWS)
            adj[plane, wide, :] = (
                c0 * w0[plane + 2, wide, :] + c1 * w1[plane + 1, wide, :] + c2 * w2[plane, wide, :]
            )
            return carry

        sweep(rows // ROWS, mix, 0)
        if 0 < plane <= layers:
            mark = marks.at[3 + len(written)]
            written.append(
                pltpu.make_async_copy(adj.at[plane, filled], adjoint.at[plane - 1], mark)
            )
            written[-1].start()
    for copy in fields:
        copy.wait()

    @pl.when(slab == 0)
    def _():
        fwd[0, PAD : PAD + rows, :] = jnp.zeros((rows, columns), jnp.float32)

    @pl.when(slab == lax.axis_size("slab") - 1)
    def _():
        fwd[layers + 1, PAD : PAD + rows, :] = jnp.zeros((rows, columns), jnp.float32)

    tall = strip * GROUP
    lane = lax.broadcasted_iota(jnp.int32, (tall, columns), 1)
    last = lane == columns - 1
    start = lane == 0

    def ahead(value):
        return jnp.where(last, 0.0, pltpu.roll(value, columns - 1, 1))

    for layer in range(layers):

        def step(at, carry, layer=layer):
            wide = pl.ds(pl.multiple_of(at * tall + PAD, PAD), tall)
            more = pl.ds(pl.multiple_of(at * tall, PAD), tall + 2 * PAD)
            f_all = fwd[layer + 1, more, :]
            a_all = adj[layer + 1, more, :]
            f = f_all[PAD : PAD + tall]
            a = a_all[PAD : PAD + tall]
            edge = (f - ahead(f)) * (a - ahead(a))
            value = edge + jnp.where(start, f * a, pltpu.roll(edge, 1, 1))
            for plane in (layer, layer + 2):
                value = value + (f - fwd[plane, wide, :]) * (a - adj[plane, wide, :])
            for shift in (PAD - 1, PAD + 1):
                span = slice(shift, shift + tall)
                value = value + (f - f_all[span]) * (a - a_all[span])
            value = -0.5 * value
            for number in range(GROUP):
                top = value[number * strip : number * strip + half]
                bottom = value[number * strip + half : (number + 1) * strip]
                block = at * GROUP + number
                keep[block, layer * half : (layer + 1) * half, :] = jnp.where(first, top, bottom)
                give[block, layer * half : (layer + 1) * half, :] = jnp.where(first, bottom, top)
            return carry

        sweep(pairs // GROUP, step, 0, PARTS)
    for copy in written:
        copy.wait()


def body(forward_field, misfit, receivers, classes, table):
    layers, rows, columns = classes.shape
    sources = lax.axis_size("src")
    count = lax.axis_size("slab")
    per_z = CORES * Y_LO
    depth = sources // per_z
    place = lax.axis_index("src")
    slab = lax.axis_index("slab")
    core = place % CORES
    blocks = depth * CORES
    strip = rows // blocks
    forward = forward_field[0]

    def struct(*shape):
        return jax.ShapeDtypeStruct(shape, jnp.float32)

    def kept(*shape):
        return pltpu.VMEM(shape, jnp.float32)

    def stay(value):
        return pltpu.with_memory_space_constraint(value, pltpu.VMEM)

    def limit(size):
        return pltpu.CompilerParams(vmem_limit_bytes=size * MIB)

    mine = (place // per_z) * CORES + core
    part = lookup(lax.dynamic_slice_in_dim(classes, mine * strip, strip, axis=1), table)
    lists = jnp.concatenate([receivers[0].T.astype(jnp.float32), misfit], axis=0)
    packed = jnp.concatenate(
        [part.reshape(layers * strip, columns), lists.reshape(3 * PIECES, columns)], axis=0
    )
    below = slab_ring(packed, 1)
    above = slab_ring(packed, -1)
    shares = jnp.stack(
        [
            jnp.where(slab > 0, below[: layers * strip], 0.0),
            jnp.where(slab < count - 1, above[: layers * strip], 0.0),
        ]
    ).reshape(2, layers, strip, columns)
    groups = [
        [z * per_z + y * CORES + c for z in range(depth) for c in range(CORES)] for y in range(Y_LO)
    ]
    halo = lax.all_gather(shares, "src", axis_index_groups=groups)

    bottom, top, below, above = lax.optimization_barrier(
        (forward[:1], forward[-1:], below, above)
    )
    lower = slab_ring(top, 1)
    upper = slab_ring(bottom, -1)

    vmem = pl.BlockSpec(memory_space=pltpu.VMEM)
    anywhere = pl.BlockSpec(memory_space=pl.ANY)
    smem = pl.BlockSpec(memory_space=pltpu.SMEM)
    deep = layers + 2 * REACH
    side, own = pl.pallas_call(
        scatter_kernel,
        out_shape=(kept(deep, rows, columns), kept(layers, rows, columns)),
        in_specs=[vmem, vmem, vmem, vmem, smem],
        compiler_params=limit(24),
        name="scatter",
    )(below, packed, above, classes, table)

    tall = rows + 2 * PAD
    thick = layers + 2
    w0, w1, w2, sums = pl.pallas_call(
        vectors_kernel,
        out_shape=(
            kept(deep, tall, columns),
            kept(deep - 2, tall, columns),
            kept(deep - 4, tall, columns),
            struct(count, 8, 128),
        ),
        in_specs=[vmem, anywhere, vmem],
        out_specs=(vmem, vmem, vmem, vmem),
        scratch_shapes=[
            pltpu.VMEM((deep + 2, tall, columns), jnp.float32),
            pltpu.VMEM((deep, rows, columns), jnp.float32),
            pltpu.VMEM((deep, tall, columns), jnp.float32),
            pltpu.VMEM((deep, rows, columns), jnp.float32),
            pltpu.VMEM((deep, rows, columns), jnp.float32),
            pltpu.SemaphoreType.DMA((2 * blocks + 1,)),
        ],
        compiler_params=limit(34),
        name="vectors",
    )(stay(own), halo, stay(side))

    sums = lax.all_to_all(sums, "slab", 0, 0)
    half = rows // sources
    adjoint, keep, give = pl.pallas_call(
        terms_kernel,
        out_shape=(struct(layers, rows, columns),) + (struct(blocks, layers * half, columns),) * 2,
        in_specs=[vmem] * 4 + [anywhere] * 3,
        out_specs=(anywhere, vmem, vmem),
        scratch_shapes=[
            pltpu.VMEM((thick, tall, columns), jnp.float32),
            pltpu.VMEM((thick, tall, columns), jnp.float32),
            pltpu.SemaphoreType.DMA((3 + layers,)),
        ],
        compiler_params=limit(16),
        name="terms",
    )(sums, stay(w0), stay(w1), stay(w2), forward, lower, upper)

    got = lax.ppermute(give, "src", [(i, i ^ 1) for i in range(sources)])
    groups = [
        [z * per_z + y * CORES + c for z in range(depth) for y in range(Y_LO)] for c in range(CORES)
    ]
    shares = lax.all_to_all(keep + got, "src", 0, 0, axis_index_groups=groups)
    gradient = jnp.sum(shares, axis=0).reshape(layers, half, columns)
    return (adjoint[None], gradient)


def solution(mesh):
    placed = (
        P("src", "slab", None, None),
        P("src", "slab"),
        P("src", "slab", None),
        P("slab", None, None),
        P(),
    )
    return jax.shard_map(
        body,
        mesh=mesh,
        in_specs=placed,
        out_specs=(P("src", "slab", None, None), P("slab", "src", None)),
        check_vma=False,
    )
```

```python
import jax
import jax.numpy as jnp
from jax import lax
from jax.experimental import pallas as pl
from jax.experimental.pallas import tpu as pltpu
from jax.sharding import PartitionSpec as P

CORES = 2
Y_LO = 2
REACH = 3
PAD = 8
ROWS = 16
UNROLL = 24
GROUP = 2
PARTS = 8
PIECES = 3
MIB = 1024 * 1024


def lookup(classes, table):
    labels = jnp.arange(table.shape[0], dtype=jnp.int32)[:, None, None, None]
    return jnp.sum(jnp.where(classes[None] == labels, table[:, None, None, None], 0.0), axis=0)


def slab_ring(value, step):
    count = lax.axis_size("slab")
    return lax.ppermute(value, "slab", [(i, (i + step) % count) for i in range(count)])


def scatter_kernel(below, own, above, classes, table, side, conduct):
    layers, rows, columns = classes.shape
    slab = lax.axis_index("slab")
    count = own.shape[1] * PIECES
    across = lax.broadcasted_iota(jnp.int32, (count, columns), 1)
    down = lax.broadcasted_iota(jnp.int32, (rows, count), 0)
    sources = (
        (below, range(layers - REACH, layers), 0),
        (own, range(layers), REACH),
        (above, range(REACH), REACH + layers),
    )
    for number, (entries, planes, start) in enumerate(sources):
        top = entries.shape[0] - 3 * PIECES
        lines = [entries[row : row + 1, :] for row in range(top, entries.shape[0])]
        first, index, value = [
            jnp.concatenate(lines[at * PIECES : (at + 1) * PIECES], axis=1) for at in range(3)
        ]
        first = first - ((slab + number - 1) * layers).astype(jnp.float32)
        line = jnp.floor((index + 0.5) * (1.0 / columns))
        place = (first * rows + line).astype(jnp.int32)
        upright = jnp.transpose(
            jnp.concatenate([index - line * columns, value] + [value * 0.0] * 6, axis=0)
        )
        hit = across == upright[:, 0:1].astype(jnp.int32)
        parts = []
        rest = upright[:, 1:2]
        for _ in range(3):
            piece = rest.astype(jnp.bfloat16).astype(jnp.float32)
            rest = rest - piece
            parts.append(jnp.where(hit, piece, 0.0).astype(jnp.bfloat16))
        parts = jnp.concatenate(parts, axis=1)
        for step, plane in enumerate(planes):
            chosen = jnp.where(down + plane * rows == place, 1.0, 0.0).astype(jnp.bfloat16)
            total = jnp.dot(chosen, parts, preferred_element_type=jnp.float32)
            side[start + step] = (
                total[:, :columns] + total[:, columns : 2 * columns] + total[:, 2 * columns :]
            )

    values = [table[label] for label in range(table.shape[0])]

    def strip(at, carry):
        at = pl.multiple_of(at * ROWS, ROWS)
        for layer in range(layers):
            conduct[layer, pl.ds(at, ROWS), :] = choose(classes[layer, pl.ds(at, ROWS), :], values)
        return carry

    sweep(rows // ROWS, strip, 0)


def choose(labels, values):
    bit = 1
    while len(values) > 1:
        high = (labels & bit) != 0
        values = [jnp.where(high, values[i + 1], values[i]) for i in range(0, len(values), 2)]
        bit *= 2
    return values[0]


def sweep(count, step, carry, unroll=None):
    unroll = unroll or UNROLL

    def several(at, inner):
        for number in range(unroll):
            inner = step(at * unroll + number, inner)
        return inner

    return lax.fori_loop(0, count // unroll, several, carry)


def reciprocal(value):
    guess = pl.reciprocal(value, approx=True)
    for _ in range(2):
        guess = guess * (2.0 - value * guess)
    return guess


def vectors_kernel(
    own, halo, right, f0, f1, f2, sums, cond, side, near_x, near_y, near_z, inverse, marks
):
    layers, rows, columns = own.shape
    blocks, _, _, strip, _ = halo.shape
    filled = pl.ds(PAD, rows)
    first_copies, copies = [], []

    def fetch(source, target, group):
        mark = marks.at[len(first_copies) + len(copies)]
        copy = pltpu.make_async_copy(source, target, mark)
        copy.start()
        group.append(copy)

    fetch(own, cond.at[pl.ds(layers, layers), filled], first_copies)
    inner = pl.ds(REACH, layers)
    fetch(right.at[inner], side.at[inner], first_copies)
    for block in range(blocks):
        for step in range(2):
            target = cond.at[pl.ds(2 * step * layers, layers), pl.ds(PAD + block * strip, strip)]
            fetch(halo.at[block, step], target, copies)
    for ends in (pl.ds(0, REACH), pl.ds(REACH + layers, REACH)):
        fetch(right.at[ends], side.at[ends], copies)
    slab = lax.axis_index("slab")
    slabs = lax.axis_size("slab")
    deep = layers + 2 * REACH
    lane = lax.broadcasted_iota(jnp.int32, (ROWS, columns), 1)
    blank = jnp.zeros((PAD, columns), jnp.float32)
    for ref in (cond, near_y, f0, f1, f2):
        for plane in range(ref.shape[0]):
            ref[plane, 0:PAD, :] = blank
            ref[plane, PAD + rows : 2 * PAD + rows, :] = blank

    def here(at):
        return pl.ds(pl.multiple_of(at * ROWS + PAD, PAD), ROWS)

    def before(at):
        return pl.ds(pl.multiple_of(at * ROWS, PAD), ROWS + PAD)

    def after(at):
        return pl.ds(pl.multiple_of(at * ROWS + PAD, PAD), ROWS + PAD)

    def plain(at):
        return pl.ds(pl.multiple_of(at * ROWS, ROWS), ROWS)

    strips = rows // ROWS

    def setup(plane, carry):
        layer = slab * layers + plane - REACH
        real = jnp.logical_and(layer >= 0, layer < slabs * layers)
        scale = jnp.where(real, 1.0, 0.0)

        def step(at, inner):
            centre = cond[plane + 1, here(at), :]
            lower = cond[plane, here(at), :]
            upper = cond[plane + 2, here(at), :]
            ahead = cond[plane + 1, after(at), :][1 : ROWS + 1]
            behind = cond[plane + 1, before(at), :][PAD - 1 : PAD - 1 + ROWS]
            right = jnp.where(lane == columns - 1, 0.0, pltpu.roll(centre, columns - 1, 1))
            left = jnp.where(lane == 0, 0.0, pltpu.roll(centre, 1, 1))
            total = 6.0 * centre + ((lower + upper) + (ahead + behind) + (left + right))
            turned = scale * reciprocal(total + (1.0 - scale))
            inverse[plane, plain(at), :] = turned
            near_x[plane, plain(at), :] = jnp.where(lane == columns - 1, 0.0, centre + right)
            near_y[plane, here(at), :] = centre + ahead
            near_z[plane, plain(at), :] = centre + upper
            f0[plane, here(at), :] = side[plane, plain(at), :] * (2.0 * turned)
            return inner

        return sweep(strips, step, carry)

    for copy in first_copies:
        copy.wait()
    lax.fori_loop(REACH + 1, REACH + layers - 1, setup, 0)
    for copy in copies:
        copy.wait()
    lax.fori_loop(0, REACH + 1, setup, 0)
    lax.fori_loop(REACH + layers - 1, deep, setup, 0)

    def spread(field, offset, plane, at):
        centre = field[plane, here(at), :]
        across = near_x[plane + offset, plain(at), :]
        total = across * pltpu.roll(centre, columns - 1, 1) + pltpu.roll(across * centre, 1, 1)
        ahead = field[plane, after(at), :][1 : ROWS + 1]
        total = total + near_y[plane + offset, here(at), :] * ahead
        behind = near_y[plane + offset, before(at), :] * field[plane, before(at), :]
        total = total + behind[PAD - 1 : PAD - 1 + ROWS]
        total = total + near_z[plane + offset, plain(at), :] * field[plane + 1, here(at), :]
        total = total + near_z[plane + offset - 1, plain(at), :] * field[plane - 1, here(at), :]
        return centre, total

    def fold(value):
        total = value[0:8]
        for start in range(8, ROWS, 8):
            total = total + value[start : start + 8]
        return total

    def outer(field, offset, target, planes):
        for plane in planes:

            def step(at, inner, plane=plane):
                _, total = spread(field, offset, plane, at)
                target[plane - 1, here(at), :] = total * inverse[plane + offset, plain(at), :]
                return inner

            sweep(strips, step, 0)

    zero = jnp.zeros((8, columns), jnp.float32)

    def inside0(plane, carry):
        def step(at, inner):
            s0, s1, s2 = inner
            centre, total = spread(f0, 0, plane, at)
            value = total * inverse[plane, plain(at), :]
            f1[plane - 1, here(at), :] = value
            return (
                s0 + fold(centre * side[plane, plain(at), :]),
                s1 + fold(centre * total),
                s2 + fold(value * total),
            )

        return sweep(strips, step, carry)

    def inside1(plane, carry):
        def step(at, inner):
            s3, s4 = inner
            centre, total = spread(f1, 1, plane, at)
            value = total * inverse[plane + 1, plain(at), :]
            f2[plane - 1, here(at), :] = value
            return s3 + fold(centre * total), s4 + fold(value * total)

        return sweep(strips, step, carry)

    def inside2(plane, carry):
        def step(at, inner):
            centre, total = spread(f2, 2, plane, at)
            return inner + fold(centre * total)

        return sweep(strips, step, carry)

    outer(f0, 0, f1, (1, 2, deep - 3, deep - 2))
    s0, s1, s2 = lax.fori_loop(REACH, REACH + layers, inside0, (zero, zero, zero))
    outer(f1, 1, f2, (1, deep - 4))
    s3, s4 = lax.fori_loop(REACH - 1, REACH - 1 + layers, inside1, (zero, zero))
    s5 = lax.fori_loop(REACH - 2, REACH - 2 + layers, inside2, zero)
    for row, total in enumerate((2.0 * s0, s1, s2, s3, s4, s5)):
        single = jnp.sum(jnp.sum(total, axis=0, keepdims=True), axis=1, keepdims=True)
        for target in range(sums.shape[0]):
            sums[target, row : row + 1, :] = jnp.broadcast_to(single, (1, sums.shape[2]))
    for target in range(sums.shape[0]):
        sums[target, 6:8, :] = jnp.zeros((2, sums.shape[2]), jnp.float32)


def weights(moments):
    m = [moments[i] / moments[0] for i in range(6)]
    g = [m[i] - m[i + 1] for i in range(5)]
    l10 = g[1] / g[0]
    l20 = g[2] / g[0]
    d1 = g[2] - l10 * g[1]
    e = g[3] - l20 * g[1]
    l21 = e / d1
    d2 = g[4] - l20 * g[2] - l21 * e
    y0 = m[0]
    y1 = m[1] - l10 * y0
    y2 = m[2] - l20 * y0 - l21 * y1
    c2 = y2 / d2
    c1 = y1 / d1 - l21 * c2
    c0 = y0 / g[0] - l10 * c1 - l20 * c2
    return c0, c1, c2


def terms_kernel(
    sums, w0, w1, w2, forward, lower, upper, adjoint, keep, give, adj, fwd, marks
):
    layers, rows, columns = forward.shape
    pairs, _, _ = keep.shape
    strip = rows // pairs
    half = strip // 2
    thick = layers + 2
    first = lax.axis_index("src") % CORES == 0
    slab = lax.axis_index("slab")
    filled = pl.ds(PAD, rows)
    fields = []
    for number, (source, start, count) in enumerate(
        ((lower, 0, 1), (forward, 1, layers), (upper, layers + 1, 1))
    ):
        target = fwd.at[pl.ds(start, count), filled]
        fields.append(pltpu.make_async_copy(source, target, marks.at[number]))
        fields[-1].start()
    blank = jnp.zeros((PAD, columns), jnp.float32)
    for ref in (adj, fwd):
        for plane in range(thick):
            ref[plane, 0:PAD, :] = blank
            ref[plane, PAD + rows : 2 * PAD + rows, :] = blank
    total = sums[0]
    for other in range(1, sums.shape[0]):
        total = total + sums[other]
    c0, c1, c2 = weights([total[i : i + 1, 0:1] for i in range(6)])
    c0, c1, c2 = [jnp.broadcast_to(c, (ROWS, columns)) for c in (c0, c1, c2)]

    written = []
    for plane in range(thick):
        def mix(at, carry, plane=plane):
            wide = pl.ds(pl.multiple_of(at * ROWS + PAD, PAD), ROWS)
            adj[plane, wide, :] = (
                c0 * w0[plane + 2, wide, :] + c1 * w1[plane + 1, wide, :] + c2 * w2[plane, wide, :]
            )
            return carry

        sweep(rows // ROWS, mix, 0)
        if 0 < plane <= layers:
            mark = marks.at[3 + len(written)]
            written.append(
                pltpu.make_async_copy(adj.at[plane, filled], adjoint.at[plane - 1], mark)
            )
            written[-1].start()
    for copy in fields:
        copy.wait()

    @pl.when(slab == 0)
    def _():
        fwd[0, PAD : PAD + rows, :] = jnp.zeros((rows, columns), jnp.float32)

    @pl.when(slab == lax.axis_size("slab") - 1)
    def _():
        fwd[layers + 1, PAD : PAD + rows, :] = jnp.zeros((rows, columns), jnp.float32)

    tall = strip * GROUP
    lane = lax.broadcasted_iota(jnp.int32, (tall, columns), 1)
    last = lane == columns - 1
    start = lane == 0

    def ahead(value):
        return jnp.where(last, 0.0, pltpu.roll(value, columns - 1, 1))

    for layer in range(layers):

        def step(at, carry, layer=layer):
            wide = pl.ds(pl.multiple_of(at * tall + PAD, PAD), tall)
            more = pl.ds(pl.multiple_of(at * tall, PAD), tall + 2 * PAD)
            f_all = fwd[layer + 1, more, :]
            a_all = adj[layer + 1, more, :]
            f = f_all[PAD : PAD + tall]
            a = a_all[PAD : PAD + tall]
            edge = (f - ahead(f)) * (a - ahead(a))
            value = edge + jnp.where(start, f * a, pltpu.roll(edge, 1, 1))
            for plane in (layer, layer + 2):
                value = value + (f - fwd[plane, wide, :]) * (a - adj[plane, wide, :])
            for shift in (PAD - 1, PAD + 1):
                span = slice(shift, shift + tall)
                value = value + (f - f_all[span]) * (a - a_all[span])
            value = -0.5 * value
            for number in range(GROUP):
                top = value[number * strip : number * strip + half]
                bottom = value[number * strip + half : (number + 1) * strip]
                block = at * GROUP + number
                keep[block, layer * half : (layer + 1) * half, :] = jnp.where(first, top, bottom)
                give[block, layer * half : (layer + 1) * half, :] = jnp.where(first, bottom, top)
            return carry

        sweep(pairs // GROUP, step, 0, PARTS)
    for copy in written:
        copy.wait()


def body(forward_field, misfit, receivers, classes, table):
    layers, rows, columns = classes.shape
    sources = lax.axis_size("src")
    count = lax.axis_size("slab")
    per_z = CORES * Y_LO
    depth = sources // per_z
    place = lax.axis_index("src")
    slab = lax.axis_index("slab")
    core = place % CORES
    blocks = depth * CORES
    strip = rows // blocks
    forward = forward_field[0]

    def struct(*shape):
        return jax.ShapeDtypeStruct(shape, jnp.float32)

    def kept(*shape):
        return pltpu.VMEM(shape, jnp.float32)

    def stay(value):
        return pltpu.with_memory_space_constraint(value, pltpu.VMEM)

    def limit(size):
        return pltpu.CompilerParams(vmem_limit_bytes=size * MIB)

    mine = (place // per_z) * CORES + core
    part = lookup(lax.dynamic_slice_in_dim(classes, mine * strip, strip, axis=1), table)
    lists = jnp.concatenate([receivers[0].T.astype(jnp.float32), misfit], axis=0)
    packed = jnp.concatenate(
        [part.reshape(layers * strip, columns), lists.reshape(3 * PIECES, columns)], axis=0
    )
    below = slab_ring(packed, 1)
    above = slab_ring(packed, -1)
    shares = jnp.stack(
        [
            jnp.where(slab > 0, below[: layers * strip], 0.0),
            jnp.where(slab < count - 1, above[: layers * strip], 0.0),
        ]
    ).reshape(2, layers, strip, columns)
    groups = [
        [z * per_z + y * CORES + c for z in range(depth) for c in range(CORES)] for y in range(Y_LO)
    ]
    halo = lax.all_gather(shares, "src", axis_index_groups=groups)

    bottom, top, below, above = lax.optimization_barrier(
        (forward[:1], forward[-1:], below, above)
    )
    lower = slab_ring(top, 1)
    upper = slab_ring(bottom, -1)

    vmem = pl.BlockSpec(memory_space=pltpu.VMEM)
    anywhere = pl.BlockSpec(memory_space=pl.ANY)
    smem = pl.BlockSpec(memory_space=pltpu.SMEM)
    deep = layers + 2 * REACH
    side, own = pl.pallas_call(
        scatter_kernel,
        out_shape=(struct(deep, rows, columns), struct(layers, rows, columns)),
        in_specs=[vmem, vmem, vmem, vmem, smem],
        compiler_params=limit(24),
        name="scatter",
    )(below, packed, above, classes, table)

    halo, lower, upper = lax.optimization_barrier((halo, lower, upper))
    tall = rows + 2 * PAD
    thick = layers + 2
    w0, w1, w2, sums = pl.pallas_call(
        vectors_kernel,
        out_shape=(
            kept(deep, tall, columns),
            kept(deep - 2, tall, columns),
            kept(deep - 4, tall, columns),
            struct(count, 8, 128),
        ),
        in_specs=[anywhere] * 3,
        out_specs=(vmem, vmem, vmem, vmem),
        scratch_shapes=[
            pltpu.VMEM((deep + 2, tall, columns), jnp.float32),
            pltpu.VMEM((deep, rows, columns), jnp.float32),
            pltpu.VMEM((deep, rows, columns), jnp.float32),
            pltpu.VMEM((deep, tall, columns), jnp.float32),
            pltpu.VMEM((deep, rows, columns), jnp.float32),
            pltpu.VMEM((deep, rows, columns), jnp.float32),
            pltpu.SemaphoreType.DMA((2 * blocks + 4,)),
        ],
        compiler_params=limit(40),
        name="vectors",
    )(own, halo, side)

    sums = lax.all_to_all(sums, "slab", 0, 0)
    half = rows // sources
    adjoint, keep, give = pl.pallas_call(
        terms_kernel,
        out_shape=(struct(layers, rows, columns),) + (struct(blocks, layers * half, columns),) * 2,
        in_specs=[vmem] * 4 + [anywhere] * 3,
        out_specs=(anywhere, vmem, vmem),
        scratch_shapes=[
            pltpu.VMEM((thick, tall, columns), jnp.float32),
            pltpu.VMEM((thick, tall, columns), jnp.float32),
            pltpu.SemaphoreType.DMA((3 + layers,)),
        ],
        compiler_params=limit(16),
        name="terms",
    )(sums, stay(w0), stay(w1), stay(w2), forward, lower, upper)

    got = lax.ppermute(give, "src", [(i, i ^ 1) for i in range(sources)])
    both = (keep + got).reshape(depth // 2, 2, Y_LO, layers * half, columns)
    parity = (place // per_z) % 2
    held = lax.dynamic_index_in_dim(both, parity, 1, keepdims=False)
    sent = lax.dynamic_index_in_dim(both, 1 - parity, 1, keepdims=False)

    def beside(value, way):
        pairs = []
        for i in range(sources):
            step = way if (i // per_z) % 2 == 0 else -way
            pairs.append((i, (i + step * per_z) % sources))
        return lax.ppermute(value, "src", pairs)

    middle = layers * half // 2
    came = [beside(sent[:, :, :middle], 1), beside(sent[:, :, middle:], -1)]
    part = (held + jnp.concatenate(came, axis=2)).reshape(blocks // 2, layers * half, columns)
    groups = [
        [z * per_z + y * CORES + c for z in range(first, depth, 2) for y in range(Y_LO)]
        for first in range(2)
        for c in range(CORES)
    ]
    shares = lax.all_to_all(part, "src", 0, 0, axis_index_groups=groups)
    gradient = jnp.sum(shares, axis=0).reshape(layers, half, columns)
    return (adjoint[None], gradient)


def solution(mesh):
    placed = (
        P("src", "slab", None, None),
        P("src", "slab"),
        P("src", "slab", None),
        P("slab", None, None),
        P(),
    )
    return jax.shard_map(
        body,
        mesh=mesh,
        in_specs=placed,
        out_specs=(P("src", "slab", None, None), P("slab", "src", None)),
        check_vma=False,
    )
```

```python
import functools

import jax
import jax.numpy as jnp
from jax import lax
from jax.experimental import pallas as pl
from jax.experimental.pallas import tpu as pltpu
from jax.sharding import PartitionSpec as P

CORES = 2
Y_LO = 2
REACH = 3
PAD = 8
ROWS = 16
UNROLL = 24
GROUP = 2
PARTS = 8
PIECES = 3
MIB = 1024 * 1024


def lookup(classes, table):
    labels = jnp.arange(table.shape[0], dtype=jnp.int32)[:, None, None, None]
    return jnp.sum(jnp.where(classes[None] == labels, table[:, None, None, None], 0.0), axis=0)


def slab_ring(value, step):
    count = lax.axis_size("slab")
    return lax.ppermute(value, "slab", [(i, (i + step) % count) for i in range(count)])


def ring_steps(depth):
    steps = [0, 1, depth // 2]
    for step in range(depth // 2 - 1, 1, -1):
        steps += [step, -step]
    return steps + [-1]


def fill(entries, start, layers, rows, columns, planes, target):
    count = entries.shape[1] * PIECES
    across = lax.broadcasted_iota(jnp.int32, (count, columns), 1)
    down = lax.broadcasted_iota(jnp.int32, (rows, count), 0)
    top = entries.shape[0] - 3 * PIECES
    lines = [entries[row : row + 1, :] for row in range(top, entries.shape[0])]
    first, index, value = [
        jnp.concatenate(lines[at * PIECES : (at + 1) * PIECES], axis=1) for at in range(3)
    ]
    first = first - (start * layers).astype(jnp.float32)
    line = jnp.floor((index + 0.5) * (1.0 / columns))
    place = (first * rows + line).astype(jnp.int32)
    upright = jnp.transpose(
        jnp.concatenate([index - line * columns, value] + [value * 0.0] * 6, axis=0)
    )
    hit = across == upright[:, 0:1].astype(jnp.int32)
    parts = []
    rest = upright[:, 1:2]
    for _ in range(3):
        piece = rest.astype(jnp.bfloat16).astype(jnp.float32)
        rest = rest - piece
        parts.append(jnp.where(hit, piece, 0.0).astype(jnp.bfloat16))
    parts = jnp.concatenate(parts, axis=1)
    for step, plane in enumerate(planes):
        chosen = jnp.where(down + plane * rows == place, 1.0, 0.0).astype(jnp.bfloat16)
        total = jnp.dot(chosen, parts, preferred_element_type=jnp.float32)
        target[step] = total[:, :columns] + total[:, columns : 2 * columns] + total[:, 2 * columns :]


def own_kernel(lists, classes, table, side, conduct):
    layers, rows, columns = classes.shape
    fill(lists, lax.axis_index("slab"), layers, rows, columns, range(layers), side)
    values = [table[label] for label in range(table.shape[0])]

    def strip(at, carry):
        at = pl.multiple_of(at * ROWS, ROWS)
        for layer in range(layers):
            conduct[layer, pl.ds(at, ROWS), :] = choose(classes[layer, pl.ds(at, ROWS), :], values)
        return carry

    sweep(rows // ROWS, strip, 0)


def ends_kernel(below, above, side_below, side_above, *, layers):
    _, rows, columns = side_below.shape
    slab = lax.axis_index("slab")
    fill(below, slab - 1, layers, rows, columns, range(layers - REACH, layers), side_below)
    fill(above, slab + 1, layers, rows, columns, range(REACH), side_above)


def choose(labels, values):
    bit = 1
    while len(values) > 1:
        high = (labels & bit) != 0
        values = [jnp.where(high, values[i + 1], values[i]) for i in range(0, len(values), 2)]
        bit *= 2
    return values[0]


def sweep(count, step, carry, unroll=None):
    unroll = unroll or UNROLL

    def several(at, inner):
        for number in range(unroll):
            inner = step(at * unroll + number, inner)
        return inner

    return lax.fori_loop(0, count // unroll, several, carry)


def reciprocal(value):
    guess = pl.reciprocal(value, approx=True)
    for _ in range(2):
        guess = guess * (2.0 - value * guess)
    return guess


def vectors_kernel(
    own, right, right_below, right_above, mine, other, below, above, below_other, above_other,
    f0, f1, f2, sums, cond, side, near_x, near_y, near_z, inverse, marks
):
    layers, rows, columns = own.shape
    depth, _, outer_layers, strip, _ = mine.shape
    inner_layers = layers - outer_layers
    filled = pl.ds(PAD, rows)
    place = lax.axis_index("src")
    core = place % CORES
    z = place // (CORES * Y_LO)
    first_copies, copies = [], []

    def fetch(source, target, group):
        mark = marks.at[len(first_copies) + len(copies)]
        copy = pltpu.make_async_copy(source, target, mark)
        copy.start()
        group.append(copy)

    def lines(start, size):
        return pl.ds(pl.multiple_of(PAD + start, PAD), size)

    fetch(own, cond.at[pl.ds(layers, layers), filled], first_copies)
    fetch(right, side.at[pl.ds(REACH, layers)], first_copies)
    half = rows // CORES
    for source, start, at in (
        (below, outer_layers, core),
        (above, 2 * layers, core),
        (below_other, outer_layers, 1 - core),
        (above_other, 2 * layers, 1 - core),
    ):
        fetch(source, cond.at[pl.ds(start, inner_layers), lines(at * half, half)], copies)
    for number, step in enumerate(ring_steps(depth)):
        origin = (z - step + depth) % depth
        for source, at in ((mine, core), (other, 1 - core)):
            block = lines((origin * CORES + at) * strip, strip)
            for way, start in enumerate((0, 2 * layers + inner_layers)):
                target = cond.at[pl.ds(start, outer_layers), block]
                fetch(source.at[number, way], target, copies)
    fetch(right_below, side.at[pl.ds(0, REACH)], copies)
    fetch(right_above, side.at[pl.ds(REACH + layers, REACH)], copies)
    slab = lax.axis_index("slab")
    slabs = lax.axis_size("slab")
    deep = layers + 2 * REACH
    lane = lax.broadcasted_iota(jnp.int32, (ROWS, columns), 1)
    blank = jnp.zeros((PAD, columns), jnp.float32)
    for ref in (cond, near_y, f0, f1, f2):
        for plane in range(ref.shape[0]):
            ref[plane, 0:PAD, :] = blank
            ref[plane, PAD + rows : 2 * PAD + rows, :] = blank

    def here(at):
        return pl.ds(pl.multiple_of(at * ROWS + PAD, PAD), ROWS)

    def before(at):
        return pl.ds(pl.multiple_of(at * ROWS, PAD), ROWS + PAD)

    def after(at):
        return pl.ds(pl.multiple_of(at * ROWS + PAD, PAD), ROWS + PAD)

    def plain(at):
        return pl.ds(pl.multiple_of(at * ROWS, ROWS), ROWS)

    strips = rows // ROWS

    def setup(plane, carry):
        layer = slab * layers + plane - REACH
        real = jnp.logical_and(layer >= 0, layer < slabs * layers)
        scale = jnp.where(real, 1.0, 0.0)

        def step(at, inner):
            centre = cond[plane + 1, here(at), :]
            lower = cond[plane, here(at), :]
            upper = cond[plane + 2, here(at), :]
            ahead = cond[plane + 1, after(at), :][1 : ROWS + 1]
            behind = cond[plane + 1, before(at), :][PAD - 1 : PAD - 1 + ROWS]
            right = jnp.where(lane == columns - 1, 0.0, pltpu.roll(centre, columns - 1, 1))
            left = jnp.where(lane == 0, 0.0, pltpu.roll(centre, 1, 1))
            total = 6.0 * centre + ((lower + upper) + (ahead + behind) + (left + right))
            turned = scale * reciprocal(total + (1.0 - scale))
            inverse[plane, plain(at), :] = turned
            near_x[plane, plain(at), :] = jnp.where(lane == columns - 1, 0.0, centre + right)
            near_y[plane, here(at), :] = centre + ahead
            near_z[plane, plain(at), :] = centre + upper
            f0[plane, here(at), :] = side[plane, plain(at), :] * (2.0 * turned)
            return inner

        return sweep(strips, step, carry)

    for copy in first_copies:
        copy.wait()
    lax.fori_loop(REACH + 1, REACH + layers - 1, setup, 0)
    for copy in copies:
        copy.wait()

    @pl.when(slab == 0)
    def _():
        cond[layers - 1, filled, :] = jnp.zeros((rows, columns), jnp.float32)

    @pl.when(slab == slabs - 1)
    def _():
        cond[2 * layers, filled, :] = jnp.zeros((rows, columns), jnp.float32)

    lax.fori_loop(0, REACH + 1, setup, 0)
    lax.fori_loop(REACH + layers - 1, deep, setup, 0)

    def spread(field, offset, plane, at):
        centre = field[plane, here(at), :]
        across = near_x[plane + offset, plain(at), :]
        total = across * pltpu.roll(centre, columns - 1, 1) + pltpu.roll(across * centre, 1, 1)
        ahead = field[plane, after(at), :][1 : ROWS + 1]
        total = total + near_y[plane + offset, here(at), :] * ahead
        behind = near_y[plane + offset, before(at), :] * field[plane, before(at), :]
        total = total + behind[PAD - 1 : PAD - 1 + ROWS]
        total = total + near_z[plane + offset, plain(at), :] * field[plane + 1, here(at), :]
        total = total + near_z[plane + offset - 1, plain(at), :] * field[plane - 1, here(at), :]
        return centre, total

    def fold(value):
        total = value[0:8]
        for start in range(8, ROWS, 8):
            total = total + value[start : start + 8]
        return total

    def outer(field, offset, target, planes):
        for plane in planes:

            def step(at, inner, plane=plane):
                _, total = spread(field, offset, plane, at)
                target[plane - 1, here(at), :] = total * inverse[plane + offset, plain(at), :]
                return inner

            sweep(strips, step, 0)

    zero = jnp.zeros((8, columns), jnp.float32)

    def inside0(plane, carry):
        def step(at, inner):
            s0, s1, s2 = inner
            centre, total = spread(f0, 0, plane, at)
            value = total * inverse[plane, plain(at), :]
            f1[plane - 1, here(at), :] = value
            return (
                s0 + fold(centre * side[plane, plain(at), :]),
                s1 + fold(centre * total),
                s2 + fold(value * total),
            )

        return sweep(strips, step, carry)

    def inside1(plane, carry):
        def step(at, inner):
            s3, s4 = inner
            centre, total = spread(f1, 1, plane, at)
            value = total * inverse[plane + 1, plain(at), :]
            f2[plane - 1, here(at), :] = value
            return s3 + fold(centre * total), s4 + fold(value * total)

        return sweep(strips, step, carry)

    def inside2(plane, carry):
        def step(at, inner):
            centre, total = spread(f2, 2, plane, at)
            return inner + fold(centre * total)

        return sweep(strips, step, carry)

    outer(f0, 0, f1, (1, 2, deep - 3, deep - 2))
    s0, s1, s2 = lax.fori_loop(REACH, REACH + layers, inside0, (zero, zero, zero))
    outer(f1, 1, f2, (1, deep - 4))
    s3, s4 = lax.fori_loop(REACH - 1, REACH - 1 + layers, inside1, (zero, zero))
    s5 = lax.fori_loop(REACH - 2, REACH - 2 + layers, inside2, zero)
    for row, total in enumerate((2.0 * s0, s1, s2, s3, s4, s5)):
        single = jnp.sum(jnp.sum(total, axis=0, keepdims=True), axis=1, keepdims=True)
        for target in range(sums.shape[0]):
            sums[target, row : row + 1, :] = jnp.broadcast_to(single, (1, sums.shape[2]))
    for target in range(sums.shape[0]):
        sums[target, 6:8, :] = jnp.zeros((2, sums.shape[2]), jnp.float32)


def weights(moments):
    m = [moments[i] / moments[0] for i in range(6)]
    g = [m[i] - m[i + 1] for i in range(5)]
    l10 = g[1] / g[0]
    l20 = g[2] / g[0]
    d1 = g[2] - l10 * g[1]
    e = g[3] - l20 * g[1]
    l21 = e / d1
    d2 = g[4] - l20 * g[2] - l21 * e
    y0 = m[0]
    y1 = m[1] - l10 * y0
    y2 = m[2] - l20 * y0 - l21 * y1
    c2 = y2 / d2
    c1 = y1 / d1 - l21 * c2
    c0 = y0 / g[0] - l10 * c1 - l20 * c2
    return c0, c1, c2


def terms_kernel(
    sums, w0, w1, w2, forward, lower, upper, adjoint, keep, give, adj, fwd, marks
):
    layers, rows, columns = forward.shape
    pairs, _, _ = keep.shape
    strip = rows // pairs
    half = strip // 2
    thick = layers + 2
    first = lax.axis_index("src") % CORES == 0
    slab = lax.axis_index("slab")
    filled = pl.ds(PAD, rows)
    fields = []
    for number, (source, start, count) in enumerate(
        ((lower, 0, 1), (forward, 1, layers), (upper, layers + 1, 1))
    ):
        target = fwd.at[pl.ds(start, count), filled]
        fields.append(pltpu.make_async_copy(source, target, marks.at[number]))
        fields[-1].start()
    blank = jnp.zeros((PAD, columns), jnp.float32)
    for ref in (adj, fwd):
        for plane in range(thick):
            ref[plane, 0:PAD, :] = blank
            ref[plane, PAD + rows : 2 * PAD + rows, :] = blank
    total = sums[0]
    for other in range(1, sums.shape[0]):
        total = total + sums[other]
    c0, c1, c2 = weights([total[i : i + 1, 0:1] for i in range(6)])
    c0, c1, c2 = [jnp.broadcast_to(c, (ROWS, columns)) for c in (c0, c1, c2)]

    written = []
    for plane in range(thick):
        def mix(at, carry, plane=plane):
            wide = pl.ds(pl.multiple_of(at * ROWS + PAD, PAD), ROWS)
            adj[plane, wide, :] = (
                c0 * w0[plane + 2, wide, :] + c1 * w1[plane + 1, wide, :] + c2 * w2[plane, wide, :]
            )
            return carry

        sweep(rows // ROWS, mix, 0)
        if 0 < plane <= layers:
            mark = marks.at[3 + len(written)]
            written.append(
                pltpu.make_async_copy(adj.at[plane, filled], adjoint.at[plane - 1], mark)
            )
            written[-1].start()
    for copy in fields:
        copy.wait()

    @pl.when(slab == 0)
    def _():
        fwd[0, PAD : PAD + rows, :] = jnp.zeros((rows, columns), jnp.float32)

    @pl.when(slab == lax.axis_size("slab") - 1)
    def _():
        fwd[layers + 1, PAD : PAD + rows, :] = jnp.zeros((rows, columns), jnp.float32)

    tall = strip * GROUP
    lane = lax.broadcasted_iota(jnp.int32, (tall, columns), 1)
    last = lane == columns - 1
    start = lane == 0

    def ahead(value):
        return jnp.where(last, 0.0, pltpu.roll(value, columns - 1, 1))

    for layer in range(layers):

        def step(at, carry, layer=layer):
            wide = pl.ds(pl.multiple_of(at * tall + PAD, PAD), tall)
            more = pl.ds(pl.multiple_of(at * tall, PAD), tall + 2 * PAD)
            f_all = fwd[layer + 1, more, :]
            a_all = adj[layer + 1, more, :]
            f = f_all[PAD : PAD + tall]
            a = a_all[PAD : PAD + tall]
            edge = (f - ahead(f)) * (a - ahead(a))
            value = edge + jnp.where(start, f * a, pltpu.roll(edge, 1, 1))
            for plane in (layer, layer + 2):
                value = value + (f - fwd[plane, wide, :]) * (a - adj[plane, wide, :])
            for shift in (PAD - 1, PAD + 1):
                span = slice(shift, shift + tall)
                value = value + (f - f_all[span]) * (a - a_all[span])
            value = -0.5 * value
            for number in range(GROUP):
                top = value[number * strip : number * strip + half]
                bottom = value[number * strip + half : (number + 1) * strip]
                block = at * GROUP + number
                keep[block, layer * half : (layer + 1) * half, :] = jnp.where(first, top, bottom)
                give[block, layer * half : (layer + 1) * half, :] = jnp.where(first, bottom, top)
            return carry

        sweep(pairs // GROUP, step, 0, PARTS)
    for copy in written:
        copy.wait()


def body(forward_field, misfit, receivers, classes, table):
    layers, rows, columns = classes.shape
    sources = lax.axis_size("src")
    count = lax.axis_size("slab")
    per_z = CORES * Y_LO
    depth = sources // per_z
    place = lax.axis_index("src")
    slab = lax.axis_index("slab")
    core = place % CORES
    blocks = depth * CORES
    strip = rows // blocks
    forward = forward_field[0]

    def struct(*shape):
        return jax.ShapeDtypeStruct(shape, jnp.float32)

    def kept(*shape):
        return pltpu.VMEM(shape, jnp.float32)

    def stay(value):
        return pltpu.with_memory_space_constraint(value, pltpu.VMEM)

    def limit(size):
        return pltpu.CompilerParams(vmem_limit_bytes=size * MIB)

    def swap(value):
        return lax.ppermute(value, "src", [(i, i ^ 1) for i in range(sources)])

    outer_layers = layers // 2
    block = (place // per_z) * CORES + core
    part = lookup(lax.dynamic_slice_in_dim(classes, block * strip, strip, axis=1), table)
    lists = jnp.concatenate([receivers[0].T.astype(jnp.float32), misfit], axis=0)
    lists = lists.reshape(3 * PIECES, columns)
    held_rows = outer_layers * strip
    below = slab_ring(
        jnp.concatenate([part[:outer_layers].reshape(held_rows, columns), lists], axis=0), 1
    )
    above = slab_ring(
        jnp.concatenate([part[outer_layers:].reshape(held_rows, columns), lists], axis=0), -1
    )
    tall_part = rows // CORES
    part = lookup(lax.dynamic_slice_in_dim(classes, core * tall_part, tall_part, axis=1), table)
    near_below = slab_ring(part[outer_layers:], 1)
    near_above = slab_ring(part[:outer_layers], -1)

    vmem = pl.BlockSpec(memory_space=pltpu.VMEM)
    anywhere = pl.BlockSpec(memory_space=pl.ANY)
    smem = pl.BlockSpec(memory_space=pltpu.SMEM)
    deep = layers + 2 * REACH
    side, own = pl.pallas_call(
        own_kernel,
        out_shape=(struct(layers, rows, columns),) * 2,
        in_specs=[vmem, vmem, smem],
        compiler_params=limit(24),
        name="own",
    )(lists, classes, table)
    below, above, side, own = lax.optimization_barrier((below, above, side, own))

    share = jnp.concatenate([below[:held_rows], above[:held_rows]], axis=0)

    def passed(value, step):
        pairs = [(i, (i + step * per_z) % sources) for i in range(sources)]
        return lax.ppermute(value, "src", pairs)

    steps = ring_steps(depth)
    pieces = {step: passed(share, step) for step in steps[1:-1]}
    below, above, pieces[1] = lax.optimization_barrier((below, above, pieces[1]))
    side_below, side_above = pl.pallas_call(
        functools.partial(ends_kernel, layers=layers),
        out_shape=(struct(REACH, rows, columns),) * 2,
        in_specs=[vmem, vmem],
        compiler_params=limit(24),
        name="ends",
    )(below, above)
    late, side_below, side_above = lax.optimization_barrier((share, side_below, side_above))
    pieces[-1] = passed(late, -1)
    pieces[0] = share
    pieces = jnp.stack([pieces[step] for step in steps]).reshape(depth, 2, outer_layers, strip, columns)
    pieces_other = swap(pieces)
    near_below_other = swap(near_below)
    near_above_other = swap(near_above)

    bottom, top, near_below, near_above = lax.optimization_barrier(
        (forward[:1], forward[-1:], near_below, near_above)
    )
    lower = slab_ring(top, 1)
    upper = slab_ring(bottom, -1)

    tall = rows + 2 * PAD
    thick = layers + 2
    w0, w1, w2, sums = pl.pallas_call(
        vectors_kernel,
        out_shape=(
            kept(deep, tall, columns),
            kept(deep - 2, tall, columns),
            kept(deep - 4, tall, columns),
            struct(count, 8, 128),
        ),
        in_specs=[anywhere] * 10,
        out_specs=(vmem, vmem, vmem, vmem),
        scratch_shapes=[
            pltpu.VMEM((deep + 2, tall, columns), jnp.float32),
            pltpu.VMEM((deep, rows, columns), jnp.float32),
            pltpu.VMEM((deep, rows, columns), jnp.float32),
            pltpu.VMEM((deep, tall, columns), jnp.float32),
            pltpu.VMEM((deep, rows, columns), jnp.float32),
            pltpu.VMEM((deep, rows, columns), jnp.float32),
            pltpu.SemaphoreType.DMA((4 * depth + 8,)),
        ],
        compiler_params=limit(40),
        name="vectors",
    )(
        own,
        side,
        side_below,
        side_above,
        pieces,
        pieces_other,
        near_below,
        near_above,
        near_below_other,
        near_above_other,
    )

    sums, lower, upper = lax.optimization_barrier((sums, lower, upper))
    sums = lax.all_to_all(sums, "slab", 0, 0)
    half = rows // sources
    adjoint, keep, give = pl.pallas_call(
        terms_kernel,
        out_shape=(struct(layers, rows, columns),) + (struct(blocks, layers * half, columns),) * 2,
        in_specs=[vmem] * 4 + [anywhere] * 3,
        out_specs=(anywhere, vmem, vmem),
        scratch_shapes=[
            pltpu.VMEM((thick, tall, columns), jnp.float32),
            pltpu.VMEM((thick, tall, columns), jnp.float32),
            pltpu.SemaphoreType.DMA((3 + layers,)),
        ],
        compiler_params=limit(16),
        name="terms",
    )(sums, stay(w0), stay(w1), stay(w2), forward, lower, upper)

    got = lax.ppermute(give, "src", [(i, i ^ 1) for i in range(sources)])
    both = (keep + got).reshape(depth // 2, 2, Y_LO, layers * half, columns)
    parity = (place // per_z) % 2
    held = lax.dynamic_index_in_dim(both, parity, 1, keepdims=False)
    sent = lax.dynamic_index_in_dim(both, 1 - parity, 1, keepdims=False)

    def beside(value, way):
        pairs = []
        for i in range(sources):
            step = way if (i // per_z) % 2 == 0 else -way
            pairs.append((i, (i + step * per_z) % sources))
        return lax.ppermute(value, "src", pairs)

    middle = layers * half // 2
    came = [beside(sent[:, :, :middle], 1), beside(sent[:, :, middle:], -1)]
    part = (held + jnp.concatenate(came, axis=2)).reshape(blocks // 2, layers * half, columns)
    groups = [
        [z * per_z + y * CORES + c for z in range(first, depth, 2) for y in range(Y_LO)]
        for first in range(2)
        for c in range(CORES)
    ]
    shares = lax.all_to_all(part, "src", 0, 0, axis_index_groups=groups)
    gradient = jnp.sum(shares, axis=0).reshape(layers, half, columns)
    return (adjoint[None], gradient)


def solution(mesh):
    placed = (
        P("src", "slab", None, None),
        P("src", "slab"),
        P("src", "slab", None),
        P("slab", None, None),
        P(),
    )
    return jax.shard_map(
        body,
        mesh=mesh,
        in_specs=placed,
        out_specs=(P("src", "slab", None, None), P("slab", "src", None)),
        check_vma=False,
    )
```

```python
import jax
import jax.numpy as jnp
from jax import lax
from jax.experimental import pallas as pl
from jax.experimental.pallas import tpu as pltpu
from jax.sharding import PartitionSpec as P

CORES = 2
Y_LO = 2
REACH = 3
PAD = 8
ROWS = 16
UNROLL = 24
GROUP = 2
PARTS = 8
PIECES = 3
MIB = 1024 * 1024


def lookup(classes, table):
    labels = jnp.arange(table.shape[0], dtype=jnp.int32)[:, None, None, None]
    return jnp.sum(jnp.where(classes[None] == labels, table[:, None, None, None], 0.0), axis=0)


def slab_ring(value, step):
    count = lax.axis_size("slab")
    return lax.ppermute(value, "slab", [(i, (i + step) % count) for i in range(count)])


def scatter_kernel(below, own, above, classes, table, side, conduct):
    layers, rows, columns = classes.shape
    slab = lax.axis_index("slab")
    count = own.shape[1] * PIECES
    across = lax.broadcasted_iota(jnp.int32, (count, columns), 1)
    down = lax.broadcasted_iota(jnp.int32, (rows, count), 0)
    sources = (
        (below, range(layers - REACH, layers), 0),
        (own, range(layers), REACH),
        (above, range(REACH), REACH + layers),
    )
    for number, (entries, planes, start) in enumerate(sources):
        top = entries.shape[0] - 3 * PIECES
        lines = [entries[row : row + 1, :] for row in range(top, entries.shape[0])]
        first, index, value = [
            jnp.concatenate(lines[at * PIECES : (at + 1) * PIECES], axis=1) for at in range(3)
        ]
        first = first - ((slab + number - 1) * layers).astype(jnp.float32)
        line = jnp.floor((index + 0.5) * (1.0 / columns))
        place = (first * rows + line).astype(jnp.int32)
        upright = jnp.transpose(
            jnp.concatenate([index - line * columns, value] + [value * 0.0] * 6, axis=0)
        )
        hit = across == upright[:, 0:1].astype(jnp.int32)
        parts = []
        rest = upright[:, 1:2]
        for _ in range(3):
            piece = rest.astype(jnp.bfloat16).astype(jnp.float32)
            rest = rest - piece
            parts.append(jnp.where(hit, piece, 0.0).astype(jnp.bfloat16))
        parts = jnp.concatenate(parts, axis=1)
        for step, plane in enumerate(planes):
            chosen = jnp.where(down + plane * rows == place, 1.0, 0.0).astype(jnp.bfloat16)
            total = jnp.dot(chosen, parts, preferred_element_type=jnp.float32)
            side[start + step] = (
                total[:, :columns] + total[:, columns : 2 * columns] + total[:, 2 * columns :]
            )

    values = [table[label] for label in range(table.shape[0])]

    def strip(at, carry):
        at = pl.multiple_of(at * ROWS, ROWS)
        for layer in range(layers):
            conduct[layer, pl.ds(at, ROWS), :] = choose(classes[layer, pl.ds(at, ROWS), :], values)
        return carry

    sweep(rows // ROWS, strip, 0)


def choose(labels, values):
    bit = 1
    while len(values) > 1:
        high = (labels & bit) != 0
        values = [jnp.where(high, values[i + 1], values[i]) for i in range(0, len(values), 2)]
        bit *= 2
    return values[0]


def sweep(count, step, carry, unroll=None):
    unroll = unroll or UNROLL

    def several(at, inner):
        for number in range(unroll):
            inner = step(at * unroll + number, inner)
        return inner

    return lax.fori_loop(0, count // unroll, several, carry)


def reciprocal(value):
    guess = pl.reciprocal(value, approx=True)
    for _ in range(2):
        guess = guess * (2.0 - value * guess)
    return guess


def vectors_kernel(
    own, halo, right, f0, f1, f2, sums, cond, side, near_x, near_y, near_z, inverse, marks
):
    layers, rows, columns = own.shape
    blocks, _, _, strip, _ = halo.shape
    filled = pl.ds(PAD, rows)
    first_copies, copies = [], []

    def fetch(source, target, group):
        mark = marks.at[len(first_copies) + len(copies)]
        copy = pltpu.make_async_copy(source, target, mark)
        copy.start()
        group.append(copy)

    fetch(own, cond.at[pl.ds(layers, layers), filled], first_copies)
    inner = pl.ds(REACH, layers)
    fetch(right.at[inner], side.at[inner], first_copies)
    for block in range(blocks):
        for step in range(2):
            target = cond.at[pl.ds(2 * step * layers, layers), pl.ds(PAD + block * strip, strip)]
            fetch(halo.at[block, step], target, copies)
    for ends in (pl.ds(0, REACH), pl.ds(REACH + layers, REACH)):
        fetch(right.at[ends], side.at[ends], copies)
    slab = lax.axis_index("slab")
    slabs = lax.axis_size("slab")
    deep = layers + 2 * REACH
    lane = lax.broadcasted_iota(jnp.int32, (ROWS, columns), 1)
    blank = jnp.zeros((PAD, columns), jnp.float32)
    for ref in (cond, near_y, f0, f1, f2):
        for plane in range(ref.shape[0]):
            ref[plane, 0:PAD, :] = blank
            ref[plane, PAD + rows : 2 * PAD + rows, :] = blank

    def here(at):
        return pl.ds(pl.multiple_of(at * ROWS + PAD, PAD), ROWS)

    def before(at):
        return pl.ds(pl.multiple_of(at * ROWS, PAD), ROWS + PAD)

    def after(at):
        return pl.ds(pl.multiple_of(at * ROWS + PAD, PAD), ROWS + PAD)

    def plain(at):
        return pl.ds(pl.multiple_of(at * ROWS, ROWS), ROWS)

    strips = rows // ROWS

    def setup(plane, carry):
        layer = slab * layers + plane - REACH
        real = jnp.logical_and(layer >= 0, layer < slabs * layers)
        scale = jnp.where(real, 1.0, 0.0)

        def step(at, inner):
            centre = cond[plane + 1, here(at), :]
            lower = cond[plane, here(at), :]
            upper = cond[plane + 2, here(at), :]
            ahead = cond[plane + 1, after(at), :][1 : ROWS + 1]
            behind = cond[plane + 1, before(at), :][PAD - 1 : PAD - 1 + ROWS]
            right = jnp.where(lane == columns - 1, 0.0, pltpu.roll(centre, columns - 1, 1))
            left = jnp.where(lane == 0, 0.0, pltpu.roll(centre, 1, 1))
            total = 6.0 * centre + ((lower + upper) + (ahead + behind) + (left + right))
            turned = scale * reciprocal(total + (1.0 - scale))
            inverse[plane, plain(at), :] = turned
            near_x[plane, plain(at), :] = jnp.where(lane == columns - 1, 0.0, centre + right)
            near_y[plane, here(at), :] = centre + ahead
            near_z[plane, plain(at), :] = centre + upper
            f0[plane, here(at), :] = side[plane, plain(at), :] * (2.0 * turned)
            return inner

        return sweep(strips, step, carry)

    for copy in first_copies:
        copy.wait()
    lax.fori_loop(REACH + 1, REACH + layers - 1, setup, 0)
    for copy in copies:
        copy.wait()
    lax.fori_loop(0, REACH + 1, setup, 0)
    lax.fori_loop(REACH + layers - 1, deep, setup, 0)

    def spread(field, offset, plane, at):
        centre = field[plane, here(at), :]
        across = near_x[plane + offset, plain(at), :]
        total = across * pltpu.roll(centre, columns - 1, 1) + pltpu.roll(across * centre, 1, 1)
        ahead = field[plane, after(at), :][1 : ROWS + 1]
        total = total + near_y[plane + offset, here(at), :] * ahead
        behind = near_y[plane + offset, before(at), :] * field[plane, before(at), :]
        total = total + behind[PAD - 1 : PAD - 1 + ROWS]
        total = total + near_z[plane + offset, plain(at), :] * field[plane + 1, here(at), :]
        total = total + near_z[plane + offset - 1, plain(at), :] * field[plane - 1, here(at), :]
        return centre, total

    def fold(value):
        total = value[0:8]
        for start in range(8, ROWS, 8):
            total = total + value[start : start + 8]
        return total

    def outer(field, offset, target, planes):
        for plane in planes:

            def step(at, inner, plane=plane):
                _, total = spread(field, offset, plane, at)
                target[plane - 1, here(at), :] = total * inverse[plane + offset, plain(at), :]
                return inner

            sweep(strips, step, 0)

    zero = jnp.zeros((8, columns), jnp.float32)

    def inside0(plane, carry):
        def step(at, inner):
            s0, s1, s2 = inner
            centre, total = spread(f0, 0, plane, at)
            value = total * inverse[plane, plain(at), :]
            f1[plane - 1, here(at), :] = value
            return (
                s0 + fold(centre * side[plane, plain(at), :]),
                s1 + fold(centre * total),
                s2 + fold(value * total),
            )

        return sweep(strips, step, carry)

    def inside1(plane, carry):
        def step(at, inner):
            s3, s4 = inner
            centre, total = spread(f1, 1, plane, at)
            value = total * inverse[plane + 1, plain(at), :]
            f2[plane - 1, here(at), :] = value
            return s3 + fold(centre * total), s4 + fold(value * total)

        return sweep(strips, step, carry)

    def inside2(plane, carry):
        def step(at, inner):
            centre, total = spread(f2, 2, plane, at)
            return inner + fold(centre * total)

        return sweep(strips, step, carry)

    outer(f0, 0, f1, (1, 2, deep - 3, deep - 2))
    s0, s1, s2 = lax.fori_loop(REACH, REACH + layers, inside0, (zero, zero, zero))
    outer(f1, 1, f2, (1, deep - 4))
    s3, s4 = lax.fori_loop(REACH - 1, REACH - 1 + layers, inside1, (zero, zero))
    s5 = lax.fori_loop(REACH - 2, REACH - 2 + layers, inside2, zero)
    for row, total in enumerate((2.0 * s0, s1, s2, s3, s4, s5)):
        single = jnp.sum(jnp.sum(total, axis=0, keepdims=True), axis=1, keepdims=True)
        for target in range(sums.shape[0]):
            sums[target, row : row + 1, :] = jnp.broadcast_to(single, (1, sums.shape[2]))
    for target in range(sums.shape[0]):
        sums[target, 6:8, :] = jnp.zeros((2, sums.shape[2]), jnp.float32)


def weights(moments):
    m = [moments[i] / moments[0] for i in range(6)]
    g = [m[i] - m[i + 1] for i in range(5)]
    l10 = g[1] / g[0]
    l20 = g[2] / g[0]
    d1 = g[2] - l10 * g[1]
    e = g[3] - l20 * g[1]
    l21 = e / d1
    d2 = g[4] - l20 * g[2] - l21 * e
    y0 = m[0]
    y1 = m[1] - l10 * y0
    y2 = m[2] - l20 * y0 - l21 * y1
    c2 = y2 / d2
    c1 = y1 / d1 - l21 * c2
    c0 = y0 / g[0] - l10 * c1 - l20 * c2
    return c0, c1, c2


def terms_kernel(
    sums, w0, w1, w2, forward, lower, upper, adjoint, keep, give, adj, fwd, marks
):
    layers, rows, columns = forward.shape
    pairs, _, _ = keep.shape
    strip = rows // pairs
    half = strip // 2
    thick = layers + 2
    first = lax.axis_index("src") % CORES == 0
    slab = lax.axis_index("slab")
    filled = pl.ds(PAD, rows)
    fields = []
    for number, (source, start, count) in enumerate(
        ((lower, 0, 1), (forward, 1, layers), (upper, layers + 1, 1))
    ):
        target = fwd.at[pl.ds(start, count), filled]
        fields.append(pltpu.make_async_copy(source, target, marks.at[number]))
        fields[-1].start()
    blank = jnp.zeros((PAD, columns), jnp.float32)
    for ref in (adj, fwd):
        for plane in range(thick):
            ref[plane, 0:PAD, :] = blank
            ref[plane, PAD + rows : 2 * PAD + rows, :] = blank
    total = sums[0]
    for other in range(1, sums.shape[0]):
        total = total + sums[other]
    c0, c1, c2 = weights([total[i : i + 1, 0:1] for i in range(6)])
    c0, c1, c2 = [jnp.broadcast_to(c, (ROWS, columns)) for c in (c0, c1, c2)]

    written = []
    for plane in range(thick):
        def mix(at, carry, plane=plane):
            wide = pl.ds(pl.multiple_of(at * ROWS + PAD, PAD), ROWS)
            adj[plane, wide, :] = (
                c0 * w0[plane + 2, wide, :] + c1 * w1[plane + 1, wide, :] + c2 * w2[plane, wide, :]
            )
            return carry

        sweep(rows // ROWS, mix, 0)
        if 0 < plane <= layers:
            mark = marks.at[3 + len(written)]
            written.append(
                pltpu.make_async_copy(adj.at[plane, filled], adjoint.at[plane - 1], mark)
            )
            written[-1].start()
    for copy in fields:
        copy.wait()

    @pl.when(slab == 0)
    def _():
        fwd[0, PAD : PAD + rows, :] = jnp.zeros((rows, columns), jnp.float32)

    @pl.when(slab == lax.axis_size("slab") - 1)
    def _():
        fwd[layers + 1, PAD : PAD + rows, :] = jnp.zeros((rows, columns), jnp.float32)

    tall = strip * GROUP
    lane = lax.broadcasted_iota(jnp.int32, (tall, columns), 1)
    last = lane == columns - 1
    start = lane == 0

    def ahead(value):
        return jnp.where(last, 0.0, pltpu.roll(value, columns - 1, 1))

    for layer in range(layers):

        def step(at, carry, layer=layer):
            wide = pl.ds(pl.multiple_of(at * tall + PAD, PAD), tall)
            more = pl.ds(pl.multiple_of(at * tall, PAD), tall + 2 * PAD)
            f_all = fwd[layer + 1, more, :]
            a_all = adj[layer + 1, more, :]
            f = f_all[PAD : PAD + tall]
            a = a_all[PAD : PAD + tall]
            edge = (f - ahead(f)) * (a - ahead(a))
            value = edge + jnp.where(start, f * a, pltpu.roll(edge, 1, 1))
            for plane in (layer, layer + 2):
                value = value + (f - fwd[plane, wide, :]) * (a - adj[plane, wide, :])
            for shift in (PAD - 1, PAD + 1):
                span = slice(shift, shift + tall)
                value = value + (f - f_all[span]) * (a - a_all[span])
            value = -0.5 * value
            for number in range(GROUP):
                top = value[number * strip : number * strip + half]
                bottom = value[number * strip + half : (number + 1) * strip]
                block = at * GROUP + number
                keep[block, layer * half : (layer + 1) * half, :] = jnp.where(first, top, bottom)
                give[block, layer * half : (layer + 1) * half, :] = jnp.where(first, bottom, top)
            return carry

        sweep(pairs // GROUP, step, 0, PARTS)
    for copy in written:
        copy.wait()


def body(forward_field, misfit, receivers, classes, table):
    layers, rows, columns = classes.shape
    sources = lax.axis_size("src")
    count = lax.axis_size("slab")
    per_z = CORES * Y_LO
    depth = sources // per_z
    place = lax.axis_index("src")
    slab = lax.axis_index("slab")
    core = place % CORES
    blocks = depth * CORES
    strip = rows // blocks
    forward = forward_field[0]

    def struct(*shape):
        return jax.ShapeDtypeStruct(shape, jnp.float32)

    def kept(*shape):
        return pltpu.VMEM(shape, jnp.float32)

    def stay(value):
        return pltpu.with_memory_space_constraint(value, pltpu.VMEM)

    def limit(size):
        return pltpu.CompilerParams(vmem_limit_bytes=size * MIB)

    mine = (place // per_z) * CORES + core
    part = lookup(lax.dynamic_slice_in_dim(classes, mine * strip, strip, axis=1), table)
    part = part.reshape(layers * strip, columns)
    below = slab_ring(part, 1)
    above = slab_ring(part, -1)
    shares = jnp.stack(
        [
            jnp.where(slab > 0, below[: layers * strip], 0.0),
            jnp.where(slab < count - 1, above[: layers * strip], 0.0),
        ]
    ).reshape(2, layers, strip, columns)
    groups = [
        [z * per_z + y * CORES + c for z in range(depth) for c in range(CORES)] for y in range(Y_LO)
    ]
    halo = lax.all_gather(shares, "src", axis_index_groups=groups)

    entries, weight, below, above = lax.optimization_barrier((receivers, misfit, below, above))
    lists = jnp.concatenate([entries[0].T.astype(jnp.float32), weight], axis=0)
    packed = lists.reshape(3 * PIECES, columns)
    below = slab_ring(packed, 1)
    above = slab_ring(packed, -1)

    bottom, top, below, above = lax.optimization_barrier(
        (forward[:1], forward[-1:], below, above)
    )
    lower = slab_ring(top, 1)
    upper = slab_ring(bottom, -1)

    vmem = pl.BlockSpec(memory_space=pltpu.VMEM)
    anywhere = pl.BlockSpec(memory_space=pl.ANY)
    smem = pl.BlockSpec(memory_space=pltpu.SMEM)
    deep = layers + 2 * REACH
    side, own = pl.pallas_call(
        scatter_kernel,
        out_shape=(struct(deep, rows, columns), struct(layers, rows, columns)),
        in_specs=[vmem, vmem, vmem, vmem, smem],
        compiler_params=limit(24),
        name="scatter",
    )(below, packed, above, classes, table)

    halo, lower, upper = lax.optimization_barrier((halo, lower, upper))
    tall = rows + 2 * PAD
    thick = layers + 2
    w0, w1, w2, sums = pl.pallas_call(
        vectors_kernel,
        out_shape=(
            kept(deep, tall, columns),
            kept(deep - 2, tall, columns),
            kept(deep - 4, tall, columns),
            struct(count, 8, 128),
        ),
        in_specs=[anywhere] * 3,
        out_specs=(vmem, vmem, vmem, vmem),
        scratch_shapes=[
            pltpu.VMEM((deep + 2, tall, columns), jnp.float32),
            pltpu.VMEM((deep, rows, columns), jnp.float32),
            pltpu.VMEM((deep, rows, columns), jnp.float32),
            pltpu.VMEM((deep, tall, columns), jnp.float32),
            pltpu.VMEM((deep, rows, columns), jnp.float32),
            pltpu.VMEM((deep, rows, columns), jnp.float32),
            pltpu.SemaphoreType.DMA((2 * blocks + 4,)),
        ],
        compiler_params=limit(40),
        name="vectors",
    )(own, halo, side)

    sums = lax.all_to_all(sums, "slab", 0, 0)
    half = rows // sources
    adjoint, keep, give = pl.pallas_call(
        terms_kernel,
        out_shape=(struct(layers, rows, columns),) + (struct(blocks, layers * half, columns),) * 2,
        in_specs=[vmem] * 4 + [anywhere] * 3,
        out_specs=(anywhere, vmem, vmem),
        scratch_shapes=[
            pltpu.VMEM((thick, tall, columns), jnp.float32),
            pltpu.VMEM((thick, tall, columns), jnp.float32),
            pltpu.SemaphoreType.DMA((3 + layers,)),
        ],
        compiler_params=limit(16),
        name="terms",
    )(sums, stay(w0), stay(w1), stay(w2), forward, lower, upper)

    got = lax.ppermute(give, "src", [(i, i ^ 1) for i in range(sources)])
    both = (keep + got).reshape(depth // 2, 2, Y_LO, layers * half, columns)
    parity = (place // per_z) % 2
    held = lax.dynamic_index_in_dim(both, parity, 1, keepdims=False)
    sent = lax.dynamic_index_in_dim(both, 1 - parity, 1, keepdims=False)

    def beside(value, way):
        pairs = []
        for i in range(sources):
            step = way if (i // per_z) % 2 == 0 else -way
            pairs.append((i, (i + step * per_z) % sources))
        return lax.ppermute(value, "src", pairs)

    middle = layers * half // 2
    came = [beside(sent[:, :, :middle], 1), beside(sent[:, :, middle:], -1)]
    part = (held + jnp.concatenate(came, axis=2)).reshape(blocks // 2, layers * half, columns)
    groups = [
        [z * per_z + y * CORES + c for z in range(first, depth, 2) for y in range(Y_LO)]
        for first in range(2)
        for c in range(CORES)
    ]
    shares = lax.all_to_all(part, "src", 0, 0, axis_index_groups=groups)
    gradient = jnp.sum(shares, axis=0).reshape(layers, half, columns)
    return (adjoint[None], gradient)


def solution(mesh):
    placed = (
        P("src", "slab", None, None),
        P("src", "slab"),
        P("src", "slab", None),
        P("slab", None, None),
        P(),
    )
    return jax.shard_map(
        body,
        mesh=mesh,
        in_specs=placed,
        out_specs=(P("src", "slab", None, None), P("slab", "src", None)),
        check_vma=False,
    )
```
